512 devices in a mesh: ctx: 32 (over z_lo, x, core), slab: 16 (over z_hi, y).
Axes of the slice: x: 4, y: 4, z: 16 (z_hi: 4, z_lo: 4; z = z_hi * 4 + z_lo), core: 2. Of those that a mesh axis runs over, the one named last changes fastest.
Arguments:
- query_in: bfloat16 [512, 65536], P('slab', 'ctx'), may hold values from -6 to 6
- key_in: bfloat16 [512, 65536], P('slab', 'ctx'), may hold values from -6 to 6
- value_in: bfloat16 [512, 65536], P('slab', 'ctx'), may hold values from -6 to 6
- grad_out: bfloat16 [512, 65536], P('slab', 'ctx'), may hold values from -6 to 6
- w_first: float32 [33, 64], replicated, may hold values from -1 to 1
- b_first: float32 [64], replicated, may hold values from -3 to 3
- frequency: float32 [64], replicated, may hold values from 2 to 12
- w_second: float32 [64, 512], P(None, 'slab'), may hold values from -0.75 to 0.75
- decay_rate: float32 [512], P('slab'), may hold values from 3.0517579e-06 to 0.03
- skip_gain: float32 [512], P('slab'), may hold values from 0.5 to 1.5
Outputs:
- grad_query: bfloat16 [512, 65536], P('slab', 'ctx')
- grad_key: bfloat16 [512, 65536], P('slab', 'ctx')
- grad_value: bfloat16 [512, 65536], P('slab', 'ctx')
- grad_first: float32 [33, 64], replicated
- grad_bias: float32 [64], replicated
- grad_freq: float32 [64], replicated
- grad_second: float32 [64, 512], P(None, 'slab')
- grad_skip: float32 [512], P('slab')
The draws below stay inside these ranges and needn't reach their ends.
All inputs are finite; a program needn't handle non-finite values.
Results may differ from the reference program's by a relative error of at most 0.011.
Values may be sent and summed in bfloat16 or wider, within the bound.
A program may use at most 128 MiB of HBM per device.

```python
import math
import jax
import jax.numpy as jnp
from jax import lax

CH = 512
ORDER = 64
BANDS = 16
L = 65536
E = 33


def draw_w_first(key, part):
    key = jax.random.fold_in(key, 11)
    key_mag = jax.random.fold_in(key, 0)
    return jax.random.uniform(key_mag, (E, ORDER), jnp.float32, -1.0, 1.0)


def draw_frequency(key, part):
    key = jax.random.fold_in(key, 23)
    logs = jax.random.uniform(key, (ORDER,), jnp.float32, jnp.log(2.0), jnp.log(12.0))
    return jnp.clip(jnp.exp(logs), 2.0, 12.0)


def shard_levels(stream_key, dims, cuts, low, high):
    factor_of, own = 1.0, jax.random.fold_in(stream_key, 6)
    for axis_at, blocks in cuts:
        draws = jnp.exp(jax.random.uniform(jax.random.fold_in(own, axis_at), (blocks,), jnp.float32, low / len(cuts), high / len(cuts)))
        factor_of = factor_of * jnp.repeat(draws, dims[axis_at] // blocks).reshape([-1 if axis == axis_at else 1 for axis in range(len(dims))])
    return factor_of


def centred(rng, shape, scale, bound, cuts=(), kind=jnp.bfloat16):
    drawn = jax.random.normal(rng, shape, jnp.float32) * scale
    if len(cuts) > 0:
        drawn = shard_levels(rng, shape, cuts, -0.22, 0.18) * drawn
    return jnp.clip(drawn, min=-bound, max=bound).astype(kind)


def setup_inputs(seed: int = 0) -> dict:
    keys = jax.random.split(jax.random.key(seed), 11)
    return {
        "query_in": centred(keys[0], (CH, L), 1.0, 6.0, ((0, 16), (1, 32))),
        "key_in": centred(keys[1], (CH, L), 1.0, 6.0, ((0, 16), (1, 32))),
        "value_in": centred(keys[2], (CH, L), 1.0, 6.0, ((0, 16), (1, 32))),
        "grad_out": centred(keys[3], (CH, L), 1.0, 6.0, ((0, 16), (1, 32))),
        "w_first": draw_w_first(jax.random.fold_in(keys[10], 71), 0),
        "b_first": jnp.clip(jax.random.uniform(keys[5], (ORDER,), jnp.float32, -3.0, 3.0), -3.0, 3.0),
        "frequency": draw_frequency(jax.random.fold_in(keys[10], 71), 0),
        "w_second": centred(keys[7], (ORDER, CH), ORDER ** -0.5, 0.75, ((1, 16),), jnp.float32),
        "decay_rate": jnp.clip(jnp.exp(math.log(0.03) - 9.1932349 * jax.random.uniform(keys[8], (CH,), jnp.float32) ** shard_levels(keys[8], (CH,), ((0, 16),), -0.2, 0.2)), 3.051757857974735e-06, 0.03),
        "skip_gain": jnp.clip(0.5 + 1.0 * jax.random.uniform(keys[9], (CH,), jnp.float32) ** shard_levels(keys[9], (CH,), ((0, 16),), -0.2, 0.2), 0.5, 1.5),
    }


two_pi = 2.0 * math.pi

def features(first_pos, pos_count, seq_len):
    time_ids = first_pos + jnp.arange(pos_count, dtype=jnp.int32)
    freq_ids = jnp.arange(1, BANDS + 1, dtype=jnp.int32)
    phase = (freq_ids[:, None] * time_ids[None, :] % seq_len).astype(jnp.float32) * (two_pi / seq_len)
    linear = (time_ids.astype(jnp.float32) / seq_len)[None, :]
    return jnp.concatenate([linear, jnp.cos(phase), jnp.sin(phase)], axis=0)

def modulation(decay, first_pos, pos_count, seq_len):
    times = (first_pos + jnp.arange(pos_count, dtype=jnp.int32)).astype(jnp.float32)
    scaling = jnp.sqrt(jnp.expm1(-2.0 * decay) / jnp.expm1(-2.0 * decay * seq_len))
    return jnp.exp(-decay[:, None] * times[None, :]) * scaling[:, None]

def reference(query_in, key_in, value_in, grad_out, w_first, b_first, frequency, w_second, decay_rate, skip_gain):
    seq_len = L
    high = lax.Precision.HIGHEST
    mixed = (key_in.astype(jnp.float32) * value_in.astype(jnp.float32)).astype(jnp.bfloat16)
    grad_mid = (grad_out.astype(jnp.float32) * query_in.astype(jnp.float32)).astype(jnp.bfloat16)
    feature_rows = features(0, seq_len, seq_len)
    pre_act = jnp.dot(w_first.T, feature_rows, precision=high) + b_first[:, None]
    hidden = jnp.sin(frequency[:, None] * pre_act)
    mod_all = modulation(decay_rate, 0, seq_len, seq_len)
    filter_vals = jnp.dot(w_second.T, hidden, precision=high) * mod_all
    groups = 8
    padded_len = 2 * seq_len

    def per_block(block):
        filt_b, mixed_b, grads_b = block
        spec_h = jnp.fft.rfft(filt_b, padded_len, axis=1)
        spec_w = jnp.fft.rfft(mixed_b.astype(jnp.float32), padded_len, axis=1)
        spec_g = jnp.fft.rfft(grads_b.astype(jnp.float32), padded_len, axis=1)
        conv_b = jnp.fft.irfft(spec_h * spec_w, padded_len, axis=1)[:, :seq_len]
        back_b = jnp.fft.irfft(jnp.conj(spec_h) * spec_g, padded_len, axis=1)[:, :seq_len]
        filt_g = jnp.fft.irfft(jnp.conj(spec_w) * spec_g, padded_len, axis=1)[:, :seq_len]
        return (conv_b, back_b, filt_g)
    shaped = (filter_vals.reshape(groups, CH // groups, seq_len), mixed.reshape(groups, CH // groups, seq_len), grad_mid.reshape(groups, CH // groups, seq_len))
    conv_out, back_raw, grad_filter = lax.map(per_block, shaped)
    conv_out = conv_out.reshape(CH, seq_len)
    back_raw = back_raw.reshape(CH, seq_len)
    grad_filter = grad_filter.reshape(CH, seq_len)
    middle = (conv_out + skip_gain[:, None] * mixed.astype(jnp.float32)).astype(jnp.bfloat16)
    grad_query = (grad_out.astype(jnp.float32) * middle.astype(jnp.float32)).astype(jnp.bfloat16)
    back_out = (back_raw + skip_gain[:, None] * grad_mid.astype(jnp.float32)).astype(jnp.bfloat16)
    grad_key = (back_out.astype(jnp.float32) * value_in.astype(jnp.float32)).astype(jnp.bfloat16)
    grad_value = (back_out.astype(jnp.float32) * key_in.astype(jnp.float32)).astype(jnp.bfloat16)
    grad_mod = grad_filter * mod_all
    grad_second = jnp.dot(hidden, grad_mod.T, precision=high)
    grad_skip = lax.optimization_barrier(jnp.sum(grad_mid.astype(jnp.float32) * mixed.astype(jnp.float32), axis=1))
    grad_hidden = jnp.dot(w_second, grad_mod, precision=high)
    grad_sin = grad_hidden * jnp.cos(frequency[:, None] * pre_act)
    grad_freq = lax.optimization_barrier(jnp.sum(grad_sin * pre_act, axis=1))
    grad_pre = grad_sin * frequency[:, None]
    grad_bias = lax.optimization_barrier(jnp.sum(grad_pre, axis=1))
    grad_first = jnp.dot(feature_rows, grad_pre.T, precision=high)
    return (grad_query, grad_key, grad_value, grad_first, grad_bias, grad_freq, grad_second, grad_skip)
```

```python
import math

import jax
import jax.numpy as jnp
import ml_dtypes
import numpy as np
from jax import lax
from jax.experimental import pallas as pl
from jax.experimental.pallas import tpu as pltpu
from jax.sharding import PartitionSpec as P

BANDS = 16
CTX = 32
SLAB = 16
CHAN = 32
PART = 2048
SEQ = CTX * PART
ROWS = 16
LANES = 128
N_ONE = SEQ // LANES
ORDER = 64
KROWS = 40
PIECE = 4

MESH = pl.DeviceIdType.MESH
f32, bf16 = jnp.float32, jnp.bfloat16


def np_parts(table, count):
    out, rest = [], np.asarray(table, np.float64)
    for _ in range(count):
        part = rest.astype(np.float32).astype(ml_dtypes.bfloat16)
        out.append(part)
        rest = rest - part.astype(np.float64)
    return out


def tables():
    k_one = np.arange(N_ONE)[:, None]
    n_one = np.arange(N_ONE)[None, :]
    phase = 2 * np.pi * (((4 * k_one + 1) * n_one) % (4 * N_ONE)) / (4 * N_ONE)
    first = np.concatenate([np.cos(phase), -np.sin(phase)], axis=0)
    n_two = np.arange(LANES)[None, :]
    turn = 2 * np.pi * (k_one + 0.25) * n_two / SEQ
    twiddle = np.concatenate([np.cos(turn), np.sin(turn)], axis=1).astype(np.float32)
    small = 2 * np.pi * ((np.arange(LANES)[:, None] * n_two) % LANES) / LANES
    cos_s, sin_s = np.cos(small), np.sin(small)
    second = np.block([[cos_s, -sin_s], [sin_s, cos_s]])
    second_inv = np.block([[cos_s, sin_s], [-sin_s, cos_s]])
    place = np.arange(PART)
    bands = np.arange(1, BANDS + 1)
    arc = 2 * np.pi * (bands[:, None] * place[None, :] % SEQ) / SEQ
    base = np.zeros((KROWS, PART))
    base[:BANDS], base[BANDS : 2 * BANDS] = np.cos(arc), np.sin(arc)
    base[2 * BANDS], base[2 * BANDS + 1] = place / SEQ, 1.0
    b_one, b_two, b_three = np_parts(base, 3)
    stacked = np.concatenate([b_one, b_two, b_one, b_three, b_two, b_one], axis=0)
    pair = np.zeros((96, PART), ml_dtypes.bfloat16)
    pair[:KROWS], pair[48 : 48 + KROWS] = b_one, b_two
    start = 2 * np.pi * (bands[None, :] * np.arange(CTX)[:, None] % CTX) / CTX
    rot = np.stack([np.cos(start), np.sin(start)], axis=1).astype(np.float32)
    rot = np.broadcast_to(rot[:, :, :, None], (CTX, 2, BANDS, LANES)).copy()
    one = lambda table: np_parts(table, 1)[0]
    return (
        one(first),
        one(first.T / SEQ),
        one(second),
        one(second_inv),
        twiddle,
        stacked,
        pair,
        rot,
    )


def dot(left, right):
    return jnp.dot(left, right, preferred_element_type=f32)


def dot_first(left, right):
    return lax.dot_general(left, right, (((0,), (0,)), ((), ())), preferred_element_type=f32)


def dot_last(left, right):
    return lax.dot_general(left, right, (((1,), (1,)), ((), ())), preferred_element_type=f32)


def high_low(value):
    high = value.astype(bf16)
    return high, (value - high.astype(f32)).astype(bf16)


def eye(count):
    rows = lax.broadcasted_iota(jnp.int32, (count, count), 0)
    return rows == lax.broadcasted_iota(jnp.int32, (count, count), 1)


def as_column(row, count):
    spread = jnp.broadcast_to(row, (count, count))
    return jnp.sum(jnp.where(eye(count), spread, 0.0), axis=1, keepdims=True)


def as_row(column, count):
    spread = jnp.broadcast_to(column, (count, count))
    return jnp.sum(jnp.where(eye(count), spread, 0.0), axis=0, keepdims=True)


def sine_cosine(quarters):
    whole = jnp.floor(quarters + 0.5)
    rest = quarters - whole
    turn = whole.astype(jnp.int32)
    angle = rest * (math.pi / 2)
    square = angle * angle
    sine = angle + angle * square * (
        -1.0 / 6 + square * (1.0 / 120 + square * (-1.0 / 5040 + square * (1.0 / 362880)))
    )
    cosine = 1.0 + square * (
        -0.5 + square * (1.0 / 24 + square * (-1.0 / 720 + square * (1.0 / 40320)))
    )
    swap = (turn & 1) == 1
    sin_val = jnp.where(swap, cosine, sine)
    cos_val = jnp.where(swap, sine, cosine)
    sin_val = jnp.where((turn & 2) == 2, -sin_val, sin_val)
    cos_val = jnp.where(((turn + 1) & 2) == 2, -cos_val, cos_val)
    return sin_val, cos_val


def main_kernel(
    query_ref,
    key_ref,
    value_ref,
    grad_ref,
    w_first_ref,
    b_first_ref,
    freq_ref,
    w_second_ref,
    decay_ref,
    skip_ref,
    first_hbm,
    first_t_hbm,
    second_hbm,
    second_inv_hbm,
    twiddle_hbm,
    stacked_hbm,
    pair_hbm,
    rot_hbm,
    mid_out,
    back_out,
    sums_out,
    first,
    first_t,
    second,
    second_inv,
    twiddle,
    stacked,
    pair,
    rot,
    flat_a,
    flat_b,
    send_mg,
    recv_mg,
    send_f,
    recv_f,
    send_gf,
    recv_gf,
    send_mb,
    recv_mb,
    weights,
    weight_stack,
    quarters,
    hidden,
    cosines,
    modul,
    both,
    spec_w,
    spec_g,
    fold_a,
    fold_b,
    grad_mod,
    grad_sin,
    pay,
    send_p,
    recv_p,
    piece,
    recv_s,
    done,
    recv_d,
    table_sem,
    send_sem,
    recv_sem,
):
    me = lax.axis_index("ctx")
    slab = lax.axis_index("slab")

    barrier = pltpu.get_barrier_semaphore()

    def greet_ctx(step, carry):
        pl.semaphore_signal(
            barrier, inc=1, device_id={"ctx": lax.rem(me + step, CTX)}, device_id_type=MESH
        )
        return carry

    def greet_slab(step, carry):
        pl.semaphore_signal(
            barrier, inc=1, device_id={"slab": lax.rem(slab + step, SLAB)}, device_id_type=MESH
        )
        return carry

    lax.fori_loop(1, CTX, greet_ctx, 0)
    lax.fori_loop(1, SLAB, greet_slab, 0)

    loads = [
        pltpu.make_async_copy(source, target, table_sem.at[at])
        for at, (source, target) in enumerate(
            [
                (rot_hbm.at[me], rot),
                (stacked_hbm, stacked),
                (first_hbm, first),
                (second_hbm, second),
                (second_inv_hbm, second_inv),
                (twiddle_hbm, twiddle),
                (first_t_hbm, first_t),
                (pair_hbm, pair),
            ]
        )
    ]
    for load in loads:
        load.start()

    def send_all(source, target, at):
        def body(step, carry):
            peer = lax.rem(me + step, CTX)
            pltpu.make_async_remote_copy(
                src_ref=source.at[peer],
                dst_ref=target.at[me],
                send_sem=send_sem.at[at],
                recv_sem=recv_sem.at[at],
                device_id={"ctx": peer},
                device_id_type=MESH,
            ).start()
            return carry

        lax.fori_loop(1, CTX, body, 0)
        pltpu.make_async_copy(source.at[me], target.at[me], recv_sem.at[at]).start()

    def wait_all(target, at):
        pltpu.make_async_copy(target, target, recv_sem.at[at]).wait()

    def wait_sent(source, count, at):
        part = source.at[pl.ds(0, count)]
        pltpu.make_async_copy(part, part, send_sem.at[at]).wait()

    skip_acc = jnp.zeros((CHAN, LANES), f32)
    for col in range(ROWS):
        lanes = pl.ds(col * LANES, LANES)
        mixed = key_ref[:, lanes].astype(f32) * value_ref[:, lanes].astype(f32)
        mixed = mixed.astype(bf16).astype(f32)
        mid = grad_ref[:, lanes].astype(f32) * query_ref[:, lanes].astype(f32)
        mid = mid.astype(bf16).astype(f32)
        flat_a[pl.ds(col, CHAN, stride=ROWS), :] = mixed
        flat_b[pl.ds(col, CHAN, stride=ROWS), :] = mid
        skip_acc = skip_acc + mixed * mid
    send_mg[:, 0] = flat_a[...].reshape(CHAN, ROWS, LANES).astype(bf16)
    send_mg[:, 1] = flat_b[...].reshape(CHAN, ROWS, LANES).astype(bf16)
    skip_row = as_row(jnp.sum(skip_acc, axis=1, keepdims=True), CHAN)

    pl.semaphore_wait(barrier, CTX + SLAB - 2)
    send_all(send_mg, recv_mg, 0)

    loads[0].wait()
    cos_at, sin_at = rot[0][:, :ORDER], rot[1][:, :ORDER]
    w_lin = w_first_ref[0:1, :]
    w_cos = w_first_ref[1 : 1 + BANDS, :]
    w_sin = w_first_ref[1 + BANDS : 1 + 2 * BANDS, :]
    start_frac = me.astype(f32) * (1.0 / CTX)
    weights[...] = jnp.zeros((KROWS, ORDER), f32)
    weights[0:BANDS, :] = w_cos * cos_at + w_sin * sin_at
    weights[BANDS : 2 * BANDS, :] = w_sin * cos_at - w_cos * sin_at
    weights[2 * BANDS : 2 * BANDS + 1, :] = w_lin
    freq_row = freq_ref[...].reshape(1, ORDER)
    weights[2 * BANDS + 1 : 2 * BANDS + 2, :] = (
        b_first_ref[...].reshape(1, ORDER) + w_lin * start_frac
    )
    scaled = weights[...] * (freq_row * (2.0 / math.pi))
    part_one = scaled.astype(bf16).astype(f32)
    rest = scaled - part_one
    part_two = rest.astype(bf16).astype(f32)
    part_three = (rest - part_two).astype(bf16).astype(f32)
    for at, part in enumerate([part_one, part_one, part_two, part_one, part_two, part_three]):
        weight_stack[at * KROWS : (at + 1) * KROWS, :] = part
    loads[1].wait()
    quarters[...] = dot_first(weight_stack[...].astype(bf16), stacked[...])
    decay_col = as_column(decay_ref[...].reshape(1, CHAN), CHAN)
    small = -2.0 * decay_col
    grown = small * (
        1.0 + small / 2 * (1.0 + small / 3 * (1.0 + small / 4 * (1.0 + small / 5 * (1.0 + small / 6))))
    )
    scaling = jnp.sqrt(grown / (jnp.exp(small * SEQ) - 1.0))
    wide = 256
    for col in range(PART // wide):
        lanes = pl.ds(col * wide, wide)
        sin_val, cos_val = sine_cosine(quarters[:, lanes])
        high, low = high_low(sin_val)
        hidden[0:ORDER, lanes] = high
        hidden[ORDER : 2 * ORDER, lanes] = low
        hidden[2 * ORDER : 3 * ORDER, lanes] = high
        cosines[:, lanes] = cos_val
        times = lax.broadcasted_iota(jnp.int32, (CHAN, wide), 1) + (me * PART + col * wide)
        modul[:, lanes] = jnp.exp(-decay_col * times.astype(f32)) * scaling
    w_high, w_low = high_low(w_second_ref[...])
    w_stack = jnp.concatenate([w_high, w_high, w_low], axis=0)
    filt = dot_first(w_stack, hidden[...]) * modul[...]
    for col in range(ROWS):
        flat_a[pl.ds(col, CHAN, stride=ROWS), :] = filt[:, col * LANES : (col + 1) * LANES]
    send_f[...] = flat_a[...].reshape(CHAN, ROWS, LANES).astype(bf16)
    send_all(send_f, recv_f, 1)

    for at in range(2, 7):
        loads[at].wait()
    wait_all(recv_mg, 0)
    both[:, 0:LANES] = recv_mg[:, 0].reshape(N_ONE, LANES)
    both[:, LANES : 2 * LANES] = recv_mg[:, 1].reshape(N_ONE, LANES)
    chunk = 256

    def turned(rows):
        return twiddle[rows, 0:LANES], twiddle[rows, LANES : 2 * LANES]

    def inverse_part(real, imag, cos_t, sin_t):
        back = dot(jnp.concatenate([real, imag], axis=1).astype(bf16), second_inv[...])
        c_real, c_imag = back[:, :LANES], back[:, LANES:]
        return (
            (c_real * cos_t - c_imag * sin_t).astype(bf16),
            (c_imag * cos_t + c_real * sin_t).astype(bf16),
        )

    def spectrum(a_real, a_imag, cos_t, sin_t):
        b_real = a_real * cos_t + a_imag * sin_t
        b_imag = a_imag * cos_t - a_real * sin_t
        return dot(jnp.concatenate([b_real, b_imag], axis=1).astype(bf16), second[...])

    for at in range(N_ONE // chunk):
        rows = pl.ds(at * chunk, chunk)
        low_rows = pl.ds(N_ONE + at * chunk, chunk)
        cos_t, sin_t = turned(rows)
        a_real = dot(first[rows, :], both[...])
        a_imag = dot(first[low_rows, :], both[...])
        w_spec = spectrum(a_real[:, :LANES], a_imag[:, :LANES], cos_t, sin_t)
        g_spec = spectrum(a_real[:, LANES:], a_imag[:, LANES:], cos_t, sin_t)
        spec_w[rows, :] = w_spec
        spec_g[rows, :] = g_spec
        w_r, w_i, g_r, g_i = w_spec[:, :LANES], w_spec[:, LANES:], g_spec[:, :LANES], g_spec[:, LANES:]
        d_real, d_imag = inverse_part(w_r * g_r + w_i * g_i, w_r * g_i - w_i * g_r, cos_t, sin_t)
        fold_a[rows, :] = d_real
        fold_a[low_rows, :] = d_imag
    send_gf[...] = dot(first_t[...], fold_a[...]).astype(bf16).reshape(CTX, ROWS, LANES)
    send_all(send_gf, recv_gf, 2)

    wait_all(recv_f, 1)
    for at in range(N_ONE // chunk):
        rows = pl.ds(at * chunk, chunk)
        low_rows = pl.ds(N_ONE + at * chunk, chunk)
        cos_t, sin_t = turned(rows)
        filt_c = recv_f[...].reshape(N_ONE, LANES)
        a_real = dot(first[rows, :], filt_c)
        a_imag = dot(first[low_rows, :], filt_c)
        h_spec = spectrum(a_real, a_imag, cos_t, sin_t)
        h_r, h_i = h_spec[:, :LANES], h_spec[:, LANES:]
        w_r, w_i = spec_w[rows, 0:LANES], spec_w[rows, LANES : 2 * LANES]
        g_r, g_i = spec_g[rows, 0:LANES], spec_g[rows, LANES : 2 * LANES]
        d_real, d_imag = inverse_part(h_r * w_r - h_i * w_i, h_r * w_i + h_i * w_r, cos_t, sin_t)
        fold_b[rows, 0:LANES] = d_real
        fold_b[low_rows, 0:LANES] = d_imag
        d_real, d_imag = inverse_part(h_r * g_r + h_i * g_i, h_r * g_i - h_i * g_r, cos_t, sin_t)
        fold_b[rows, LANES : 2 * LANES] = d_real
        fold_b[low_rows, LANES : 2 * LANES] = d_imag
    spread = lax.broadcasted_iota(jnp.int32, (1, CHAN), 1)
    my_skip = jnp.sum(
        jnp.where(spread == me, skip_ref[...].reshape(1, CHAN), 0.0), axis=1, keepdims=True
    )
    direct = dot(first_t[...], fold_b[...]) + my_skip * both[...].astype(f32)
    send_mb[:, 0] = direct[:, :LANES].astype(bf16).reshape(CTX, ROWS, LANES)
    send_mb[:, 1] = direct[:, LANES:].astype(bf16).reshape(CTX, ROWS, LANES)
    send_all(send_mb, recv_mb, 3)

    wait_all(recv_gf, 2)
    flat_a[...] = recv_gf[...].astype(f32).reshape(N_ONE, LANES)
    for col in range(ROWS):
        lanes = pl.ds(col * LANES, LANES)
        part = flat_a[pl.ds(col, CHAN, stride=ROWS), :] * modul[:, lanes]
        high, low = high_low(part)
        grad_mod[0:CHAN, lanes] = high
        grad_mod[CHAN : 2 * CHAN, lanes] = low
    gm_high, gm_low = grad_mod[0:CHAN, :], grad_mod[CHAN : 2 * CHAN, :]
    w_pair = jnp.concatenate([w_high, w_low], axis=0)
    wide_part = dot(w_pair, gm_high)
    grad_hidden = wide_part[:ORDER] + wide_part[ORDER:] + dot(w_high, gm_low)
    high, low = high_low(grad_hidden * cosines[...])
    grad_sin[0:ORDER, :] = high
    grad_sin[ORDER : 2 * ORDER, :] = low
    second_part = dot_last(hidden[0 : 2 * ORDER, :], gm_high)
    second_part = (
        second_part[:ORDER] + second_part[ORDER:] + dot_last(hidden[0:ORDER, :], gm_low)
    )
    loads[7].wait()
    proj = dot_last(pair[...], grad_sin[0:ORDER, :])
    proj = proj[0:KROWS] + proj[48 : 48 + KROWS] + dot_last(pair[0:48, :], grad_sin[ORDER:, :])[0:KROWS]
    p_cos, p_sin = proj[0:BANDS], proj[BANDS : 2 * BANDS]
    p_lin, p_one = proj[2 * BANDS : 2 * BANDS + 1], proj[2 * BANDS + 1 : 2 * BANDS + 2]
    pay[...] = jnp.zeros((CTX * PIECE, LANES), f32)
    pay[0:1, 0:ORDER] = (p_lin + start_frac * p_one) * freq_row
    pay[1 : 1 + BANDS, 0:ORDER] = (p_cos * cos_at - p_sin * sin_at) * freq_row
    pay[1 + BANDS : 1 + 2 * BANDS, 0:ORDER] = (p_cos * sin_at + p_sin * cos_at) * freq_row
    pay[33:34, 0:ORDER] = p_one * freq_row
    pay[34:35, 0:ORDER] = jnp.sum(proj * weights[...], axis=0, keepdims=True)
    pay[40 : 40 + ORDER, 0:CHAN] = second_part
    pay[104:105, 0:CHAN] = skip_row

    for at in range(CTX):
        send_p[at] = pay[at * PIECE : (at + 1) * PIECE, :]
    send_all(send_p, recv_p, 4)
    wait_all(recv_p, 4)
    own = recv_p[0]
    for at in range(1, CTX):
        own = own + recv_p[at]
    piece[...] = own

    def send_slab(step, carry):
        peer = lax.rem(slab + step, SLAB)
        pltpu.make_async_remote_copy(
            src_ref=piece,
            dst_ref=recv_s.at[slab],
            send_sem=send_sem.at[5],
            recv_sem=recv_sem.at[5],
            device_id={"slab": peer},
            device_id_type=MESH,
        ).start()
        return carry

    lax.fori_loop(1, SLAB, send_slab, 0)
    pltpu.make_async_copy(piece, recv_s.at[slab], recv_sem.at[5]).start()

    wait_all(recv_mb, 3)
    flat_a[...] = recv_mb[:, 0].astype(f32).reshape(N_ONE, LANES)
    flat_b[...] = recv_mb[:, 1].astype(f32).reshape(N_ONE, LANES)
    for col in range(ROWS):
        lanes = pl.ds(col * LANES, LANES)
        mid_out[:, lanes] = flat_a[pl.ds(col, CHAN, stride=ROWS), :].astype(bf16)
        back_out[:, lanes] = flat_b[pl.ds(col, CHAN, stride=ROWS), :].astype(bf16)

    wait_all(recv_s, 5)
    total = recv_s[0]
    for at in range(1, SLAB):
        total = total + recv_s[at]
    done[...] = jnp.where(me < 10, total, piece[...])

    def send_done(step, carry):
        peer = lax.rem(me + step, CTX)
        pltpu.make_async_remote_copy(
            src_ref=done,
            dst_ref=recv_d.at[me],
            send_sem=send_sem.at[6],
            recv_sem=recv_sem.at[6],
            device_id={"ctx": peer},
            device_id_type=MESH,
        ).start()
        return carry

    lax.fori_loop(1, CTX, send_done, 0)
    pltpu.make_async_copy(done, recv_d.at[me], recv_sem.at[6]).start()

    wait_sent(send_mg, CTX - 1, 0)
    wait_sent(send_f, CTX - 1, 1)
    wait_sent(send_gf, CTX - 1, 2)
    wait_sent(send_mb, CTX - 1, 3)
    wait_sent(send_p, CTX - 1, 4)
    wait_sent(recv_s, SLAB - 1, 5)
    wait_all(recv_d, 6)
    for at in range(CTX):
        sums_out[at * PIECE : (at + 1) * PIECE, :] = recv_d[at]
    wait_sent(recv_d, CTX - 1, 6)


def last_kernel(
    key_ref,
    value_ref,
    grad_ref,
    mid_ref,
    back_ref,
    sums_ref,
    query_out,
    key_out,
    value_out,
    first_out,
    bias_out,
    freq_out,
    second_out,
    skip_out,
):
    back = back_ref[...].astype(f32)
    query_out[...] = (grad_ref[...].astype(f32) * mid_ref[...].astype(f32)).astype(bf16)
    key_out[...] = (back * value_ref[...].astype(f32)).astype(bf16)
    value_out[...] = (back * key_ref[...].astype(f32)).astype(bf16)
    first_out[...] = sums_ref[0:33, 0:ORDER]
    bias_out[...] = sums_ref[33:34, 0:ORDER].reshape(ORDER)
    freq_out[...] = sums_ref[34:35, 0:ORDER].reshape(ORDER)
    second_out[...] = sums_ref[40 : 40 + ORDER, 0:CHAN]
    skip_out[...] = sums_ref[104:105, 0:CHAN].reshape(CHAN)


def shards(
    query_in,
    key_in,
    value_in,
    grad_out,
    w_first,
    b_first,
    frequency,
    w_second,
    decay_rate,
    skip_gain,
):
    consts = tables()
    vmem = pl.BlockSpec(memory_space=pltpu.VMEM)
    anywhere = pl.BlockSpec(memory_space=pl.ANY)
    block = lambda *dims: pltpu.VMEM(dims, bf16)
    wide = lambda *dims: pltpu.VMEM(dims, f32)
    blocks = (CTX, ROWS, LANES)
    pairs = (CTX, 2, ROWS, LANES)
    rows = jax.ShapeDtypeStruct((CHAN, PART), bf16)
    mid, back, sums = pl.pallas_call(
        main_kernel,
        name="hyena_backward",
        out_shape=(rows, rows, jax.ShapeDtypeStruct((CTX * PIECE, LANES), f32)),
        in_specs=[vmem] * 10 + [anywhere] * 8,
        out_specs=(vmem, vmem, vmem),
        scratch_shapes=[
            block(2 * N_ONE, N_ONE),
            block(N_ONE, 2 * N_ONE),
            block(2 * LANES, 2 * LANES),
            block(2 * LANES, 2 * LANES),
            wide(N_ONE, 2 * LANES),
            block(6 * KROWS, PART),
            block(96, PART),
            wide(2, BANDS, LANES),
            wide(N_ONE, LANES),
            wide(N_ONE, LANES),
            block(*pairs),
            block(*pairs),
            block(*blocks),
            block(*blocks),
            block(*blocks),
            block(*blocks),
            block(*pairs),
            block(*pairs),
            wide(KROWS, ORDER),
            wide(6 * KROWS, ORDER),
            wide(ORDER, PART),
            block(3 * ORDER, PART),
            wide(ORDER, PART),
            wide(CHAN, PART),
            block(N_ONE, 2 * LANES),
            wide(N_ONE, 2 * LANES),
            wide(N_ONE, 2 * LANES),
            block(2 * N_ONE, LANES),
            block(2 * N_ONE, 2 * LANES),
            block(2 * CHAN, PART),
            block(2 * ORDER, PART),
            wide(CTX * PIECE, LANES),
            wide(CTX, PIECE, LANES),
            wide(CTX, PIECE, LANES),
            wide(PIECE, LANES),
            wide(SLAB, PIECE, LANES),
            wide(PIECE, LANES),
            wide(CTX, PIECE, LANES),
            pltpu.SemaphoreType.DMA((8,)),
            pltpu.SemaphoreType.DMA((7,)),
            pltpu.SemaphoreType.DMA((7,)),
        ],
        compiler_params=pltpu.CompilerParams(
            collective_id=0, has_side_effects=True, vmem_limit_bytes=40 * 1024 * 1024
        ),
    )(
        query_in,
        key_in,
        value_in,
        grad_out,
        w_first,
        b_first,
        frequency,
        w_second,
        decay_rate,
        skip_gain,
        *consts,
    )
    return tuple(
        pl.pallas_call(
            last_kernel,
            name="gate_products",
            out_shape=(
                rows,
                rows,
                rows,
                jax.ShapeDtypeStruct((33, ORDER), f32),
                jax.ShapeDtypeStruct((ORDER,), f32),
                jax.ShapeDtypeStruct((ORDER,), f32),
                jax.ShapeDtypeStruct((ORDER, CHAN), f32),
                jax.ShapeDtypeStruct((CHAN,), f32),
            ),
            in_specs=[vmem] * 6,
            out_specs=tuple([vmem] * 8),
        )(key_in, value_in, grad_out, mid, back, sums)
    )


def solution(mesh):
    placed = (
        P("slab", "ctx"),
        P("slab", "ctx"),
        P("slab", "ctx"),
        P("slab", "ctx"),
        P(),
        P(),
        P(),
        P(None, "slab"),
        P("slab"),
        P("slab"),
    )
    return jax.shard_map(
        shards,
        mesh=mesh,
        in_specs=placed,
        out_specs=(
            P("slab", "ctx"),
            P("slab", "ctx"),
            P("slab", "ctx"),
            P(),
            P(),
            P(),
            P(None, "slab"),
            P("slab"),
        ),
        check_vma=False,
    )
```

```python
import math

import jax
import jax.numpy as jnp
import ml_dtypes
import numpy as np
from jax import lax
from jax.experimental import pallas as pl
from jax.experimental.pallas import tpu as pltpu
from jax.sharding import PartitionSpec as P

BANDS = 16
CTX = 32
SLAB = 16
CHAN = 32
PART = 2048
SEQ = CTX * PART
ROWS = 16
LANES = 128
N_ONE = SEQ // LANES
ORDER = 64
KROWS = 40
PIECE = 2

MESH = pl.DeviceIdType.MESH
f32, bf16 = jnp.float32, jnp.bfloat16


def np_parts(table, count):
    out, rest = [], np.asarray(table, np.float64)
    for _ in range(count):
        part = rest.astype(np.float32).astype(ml_dtypes.bfloat16)
        out.append(part)
        rest = rest - part.astype(np.float64)
    return out


def tables():
    k_one = np.arange(N_ONE)[:, None]
    n_one = np.arange(N_ONE)[None, :]
    phase = 2 * np.pi * (((4 * k_one + 1) * n_one) % (4 * N_ONE)) / (4 * N_ONE)
    first = np.concatenate([np.cos(phase), -np.sin(phase)], axis=0)
    n_two = np.arange(LANES)[None, :]
    turn = 2 * np.pi * (k_one + 0.25) * n_two / SEQ
    twiddle = np.concatenate([np.cos(turn), np.sin(turn)], axis=1).astype(np.float32)
    small = 2 * np.pi * ((np.arange(LANES)[:, None] * n_two) % LANES) / LANES
    cos_s, sin_s = np.cos(small), np.sin(small)
    second = np.block([[cos_s, -sin_s], [sin_s, cos_s]])
    second_inv = np.block([[cos_s, sin_s], [-sin_s, cos_s]])
    place = np.arange(PART)
    bands = np.arange(1, BANDS + 1)
    arc = 2 * np.pi * (bands[:, None] * place[None, :] % SEQ) / SEQ
    base = np.zeros((KROWS, PART))
    base[:BANDS], base[BANDS : 2 * BANDS] = np.cos(arc), np.sin(arc)
    base[2 * BANDS], base[2 * BANDS + 1] = place / SEQ, 1.0
    b_one, b_two, b_three = np_parts(base, 3)
    stacked = np.concatenate([b_one, b_two, b_one, b_three, b_two, b_one], axis=0)
    pair = np.zeros((96, PART), ml_dtypes.bfloat16)
    pair[:KROWS], pair[48 : 48 + KROWS] = b_one, b_two
    start = 2 * np.pi * (bands[None, :] * np.arange(CTX)[:, None] % CTX) / CTX
    rot = np.stack([np.cos(start), np.sin(start)], axis=1).astype(np.float32)
    rot = np.broadcast_to(rot[:, :, :, None], (CTX, 2, BANDS, LANES)).copy()
    one = lambda table: np_parts(table, 1)[0]
    return (
        one(first),
        one(first.T / SEQ),
        one(second),
        one(second_inv),
        twiddle,
        stacked,
        pair,
        rot,
    )


def dot(left, right):
    return jnp.dot(left, right, preferred_element_type=f32)


def dot_first(left, right):
    return lax.dot_general(left, right, (((0,), (0,)), ((), ())), preferred_element_type=f32)


def dot_last(left, right):
    return lax.dot_general(left, right, (((1,), (1,)), ((), ())), preferred_element_type=f32)


def high_low(value):
    high = value.astype(bf16)
    return high, (value - high.astype(f32)).astype(bf16)


def eye(count):
    rows = lax.broadcasted_iota(jnp.int32, (count, count), 0)
    return rows == lax.broadcasted_iota(jnp.int32, (count, count), 1)


def as_column(row, count):
    spread = jnp.broadcast_to(row, (count, count))
    return jnp.sum(jnp.where(eye(count), spread, 0.0), axis=1, keepdims=True)


def in_upper_lanes(column, count):
    rows = lax.broadcasted_iota(jnp.int32, (count, LANES), 0)
    lanes = lax.broadcasted_iota(jnp.int32, (count, LANES), 1)
    spread = jnp.broadcast_to(column, (count, LANES))
    return jnp.sum(jnp.where(lanes == rows + ORDER, spread, 0.0), axis=0, keepdims=True)


def sine_cosine(quarters):
    whole = jnp.floor(quarters + 0.5)
    rest = quarters - whole
    turn = whole.astype(jnp.int32)
    angle = rest * (math.pi / 2)
    square = angle * angle
    sine = angle + angle * square * (
        -1.0 / 6 + square * (1.0 / 120 + square * (-1.0 / 5040 + square * (1.0 / 362880)))
    )
    cosine = 1.0 + square * (
        -0.5 + square * (1.0 / 24 + square * (-1.0 / 720 + square * (1.0 / 40320)))
    )
    swap = (turn & 1) == 1
    sin_val = jnp.where(swap, cosine, sine)
    cos_val = jnp.where(swap, sine, cosine)
    sin_val = jnp.where((turn & 2) == 2, -sin_val, sin_val)
    cos_val = jnp.where(((turn + 1) & 2) == 2, -cos_val, cos_val)
    return sin_val, cos_val


def main_kernel(
    query_hbm,
    key_hbm,
    value_hbm,
    grad_hbm,
    w_first_hbm,
    b_first_hbm,
    freq_hbm,
    w_second_hbm,
    decay_hbm,
    skip_hbm,
    first_hbm,
    first_t_hbm,
    second_hbm,
    second_inv_hbm,
    twiddle_hbm,
    stacked_hbm,
    pair_hbm,
    rot_hbm,
    query_out,
    key_out,
    value_out,
    sums_out,
    query_ref,
    key_ref,
    value_ref,
    grad_ref,
    w_first_ref,
    b_first_ref,
    freq_ref,
    w_second_ref,
    decay_ref,
    skip_ref,
    first,
    first_t,
    second,
    second_inv,
    twiddle,
    stacked,
    pair,
    rot,
    flat_a,
    flat_b,
    send_mg,
    recv_mg,
    send_f,
    recv_f,
    send_gf,
    recv_gf,
    send_mb,
    recv_mb,
    weights,
    weight_stack,
    quarters,
    hidden,
    cosines,
    modul,
    both,
    spec_w,
    spec_g,
    fold_a,
    fold_b,
    grad_mod,
    grad_sin,
    pay,
    send_p,
    recv_p,
    piece,
    recv_s,
    done,
    recv_d,
    table_sem,
    send_sem,
    recv_sem,
):
    me = lax.axis_index("ctx")
    slab = lax.axis_index("slab")

    barrier = pltpu.get_barrier_semaphore()

    def greet_ctx(step, carry):
        pl.semaphore_signal(
            barrier, inc=1, device_id={"ctx": lax.rem(me + step, CTX)}, device_id_type=MESH
        )
        return carry

    def greet_slab(step, carry):
        pl.semaphore_signal(
            barrier, inc=1, device_id={"slab": lax.rem(slab + step, SLAB)}, device_id_type=MESH
        )
        return carry

    lax.fori_loop(1, SLAB, greet_slab, 0)
    lax.fori_loop(1, CTX, greet_ctx, 0)

    def load(source, target, at):
        copy = pltpu.make_async_copy(source, target, table_sem.at[at])
        copy.start()
        return copy

    gates = [
        load(source, target, at)
        for at, (source, target) in enumerate(
            [(key_hbm, key_ref), (value_hbm, value_ref), (grad_hbm, grad_ref), (query_hbm, query_ref)]
        )
    ]
    layers = [
        load(source, target, 4 + at)
        for at, (source, target) in enumerate(
            [
                (rot_hbm.at[me], rot),
                (w_first_hbm, w_first_ref),
                (b_first_hbm, b_first_ref),
                (freq_hbm, freq_ref),
                (w_second_hbm, w_second_ref),
                (decay_hbm, decay_ref),
                (skip_hbm, skip_ref),
                (stacked_hbm, stacked),
            ]
        )
    ]
    transforms = [
        load(source, target, 12 + at)
        for at, (source, target) in enumerate(
            [
                (first_hbm, first),
                (second_hbm, second),
                (second_inv_hbm, second_inv),
                (twiddle_hbm, twiddle),
                (first_t_hbm, first_t),
                (pair_hbm, pair),
            ]
        )
    ]

    def wait_loads(copies):
        for copy in copies:
            copy.wait()

    def send_all(source, target, at):
        def body(step, carry):
            peer = lax.rem(me + step, CTX)
            pltpu.make_async_remote_copy(
                src_ref=source.at[peer],
                dst_ref=target.at[me],
                send_sem=send_sem.at[at],
                recv_sem=recv_sem.at[at],
                device_id={"ctx": peer},
                device_id_type=MESH,
            ).start()
            return carry

        lax.fori_loop(1, CTX, body, 0)
        pltpu.make_async_copy(source.at[me], target.at[me], recv_sem.at[at]).start()

    def wait_all(target, at):
        pltpu.make_async_copy(target, target, recv_sem.at[at]).wait()

    def wait_sent(source, count, at):
        part = source.at[pl.ds(0, count)]
        pltpu.make_async_copy(part, part, send_sem.at[at]).wait()

    wait_loads(gates)
    skip_acc = jnp.zeros((CHAN, LANES), f32)
    for col in range(ROWS):
        lanes = pl.ds(col * LANES, LANES)
        mixed = key_ref[:, lanes].astype(f32) * value_ref[:, lanes].astype(f32)
        mixed = mixed.astype(bf16).astype(f32)
        mid = grad_ref[:, lanes].astype(f32) * query_ref[:, lanes].astype(f32)
        mid = mid.astype(bf16).astype(f32)
        flat_a[pl.ds(col, CHAN, stride=ROWS), :] = mixed
        flat_b[pl.ds(col, CHAN, stride=ROWS), :] = mid
        skip_acc = skip_acc + mixed * mid
    send_mg[:, 0] = flat_a[...].reshape(CHAN, ROWS, LANES).astype(bf16)
    send_mg[:, 1] = flat_b[...].reshape(CHAN, ROWS, LANES).astype(bf16)
    skip_row = in_upper_lanes(jnp.sum(skip_acc, axis=1, keepdims=True), CHAN)

    wait_loads(layers)
    cos_at, sin_at = rot[0][:, :ORDER], rot[1][:, :ORDER]
    w_lin = w_first_ref[0:1, :]
    w_cos = w_first_ref[1 : 1 + BANDS, :]
    w_sin = w_first_ref[1 + BANDS : 1 + 2 * BANDS, :]
    start_frac = me.astype(f32) * (1.0 / CTX)
    weights[...] = jnp.zeros((KROWS, ORDER), f32)
    weights[0:BANDS, :] = w_cos * cos_at + w_sin * sin_at
    weights[BANDS : 2 * BANDS, :] = w_sin * cos_at - w_cos * sin_at
    weights[2 * BANDS : 2 * BANDS + 1, :] = w_lin
    freq_row = freq_ref[...].reshape(1, ORDER)
    weights[2 * BANDS + 1 : 2 * BANDS + 2, :] = (
        b_first_ref[...].reshape(1, ORDER) + w_lin * start_frac
    )
    scaled = weights[...] * (freq_row * (2.0 / math.pi))
    part_one = scaled.astype(bf16).astype(f32)
    rest = scaled - part_one
    part_two = rest.astype(bf16).astype(f32)
    part_three = (rest - part_two).astype(bf16).astype(f32)
    for at, part in enumerate([part_one, part_one, part_two, part_one, part_two, part_three]):
        weight_stack[at * KROWS : (at + 1) * KROWS, :] = part
    quarters[...] = dot_first(weight_stack[...].astype(bf16), stacked[...])
    decay_col = as_column(decay_ref[...].reshape(1, CHAN), CHAN)
    small = -2.0 * decay_col
    grown = small * (
        1.0 + small / 2 * (1.0 + small / 3 * (1.0 + small / 4 * (1.0 + small / 5 * (1.0 + small / 6))))
    )
    scaling = jnp.sqrt(grown / (jnp.exp(small * SEQ) - 1.0))
    wide = 256
    for col in range(PART // wide):
        lanes = pl.ds(col * wide, wide)
        sin_val, cos_val = sine_cosine(quarters[:, lanes])
        high, low = high_low(sin_val)
        hidden[0:ORDER, lanes] = high
        hidden[ORDER : 2 * ORDER, lanes] = low
        cosines[:, lanes] = cos_val
        times = lax.broadcasted_iota(jnp.int32, (CHAN, wide), 1) + (me * PART + col * wide)
        modul[:, lanes] = jnp.exp(-decay_col * times.astype(f32)) * scaling
    w_high, w_low = high_low(w_second_ref[...])
    filt = dot(jnp.concatenate([w_high, w_low], axis=0), hidden[0:ORDER, :])
    filt = filt[:CHAN] + filt[CHAN:] + dot(w_high, hidden[ORDER : 2 * ORDER, :])
    filt = filt * modul[...]
    for col in range(ROWS):
        flat_a[pl.ds(col, CHAN, stride=ROWS), :] = filt[:, col * LANES : (col + 1) * LANES]
    send_f[...] = flat_a[...].reshape(CHAN, ROWS, LANES).astype(bf16)

    pl.semaphore_wait(barrier, CTX + SLAB - 2)
    send_all(send_mg, recv_mg, 0)

    wait_loads(transforms)
    wait_all(recv_mg, 0)
    both[:, 0:LANES] = recv_mg[:, 0].reshape(N_ONE, LANES)
    both[:, LANES : 2 * LANES] = recv_mg[:, 1].reshape(N_ONE, LANES)
    chunk = 256

    def turned(rows):
        return twiddle[rows, 0:LANES], twiddle[rows, LANES : 2 * LANES]

    def inverse_part(real, imag, cos_t, sin_t):
        back = dot(jnp.concatenate([real, imag], axis=1).astype(bf16), second_inv[...])
        c_real, c_imag = back[:, :LANES], back[:, LANES:]
        return (
            (c_real * cos_t - c_imag * sin_t).astype(bf16),
            (c_imag * cos_t + c_real * sin_t).astype(bf16),
        )

    def spectrum(a_real, a_imag, cos_t, sin_t):
        b_real = a_real * cos_t + a_imag * sin_t
        b_imag = a_imag * cos_t - a_real * sin_t
        return dot(jnp.concatenate([b_real, b_imag], axis=1).astype(bf16), second[...])

    for at in range(N_ONE // chunk):
        rows = pl.ds(at * chunk, chunk)
        low_rows = pl.ds(N_ONE + at * chunk, chunk)
        cos_t, sin_t = turned(rows)
        a_real = dot(first[rows, :], both[...])
        a_imag = dot(first[low_rows, :], both[...])
        w_spec = spectrum(a_real[:, :LANES], a_imag[:, :LANES], cos_t, sin_t)
        g_spec = spectrum(a_real[:, LANES:], a_imag[:, LANES:], cos_t, sin_t)
        spec_w[rows, :] = w_spec
        spec_g[rows, :] = g_spec
        w_r, w_i, g_r, g_i = w_spec[:, :LANES], w_spec[:, LANES:], g_spec[:, :LANES], g_spec[:, LANES:]
        d_real, d_imag = inverse_part(w_r * g_r + w_i * g_i, w_r * g_i - w_i * g_r, cos_t, sin_t)
        fold_a[rows, :] = d_real
        fold_a[low_rows, :] = d_imag
    send_gf[...] = dot(first_t[...], fold_a[...]).astype(bf16).reshape(CTX, ROWS, LANES)
    send_all(send_gf, recv_gf, 2)
    send_all(send_f, recv_f, 1)

    wait_all(recv_gf, 2)
    flat_a[...] = recv_gf[...].astype(f32).reshape(N_ONE, LANES)
    for col in range(ROWS):
        lanes = pl.ds(col * LANES, LANES)
        part = flat_a[pl.ds(col, CHAN, stride=ROWS), :] * modul[:, lanes]
        high, low = high_low(part)
        grad_mod[0:CHAN, lanes] = high
        grad_mod[CHAN : 2 * CHAN, lanes] = low
        grad_mod[2 * CHAN : 3 * CHAN, lanes] = high
    grad_hidden = dot_first(jnp.concatenate([w_high, w_high, w_low], axis=0), grad_mod[...])
    high, low = high_low(grad_hidden * cosines[...])
    grad_sin[0:ORDER, :] = high
    grad_sin[ORDER : 2 * ORDER, :] = low
    second_part = dot_last(grad_mod[0 : 2 * CHAN, :], hidden[...])
    high_part = second_part[:CHAN]
    low_part = jnp.where(
        lax.broadcasted_iota(jnp.int32, (CHAN, LANES), 1) < ORDER, second_part[CHAN:], 0.0
    )
    second_part = high_part + low_part
    second_part = second_part + pltpu.roll(second_part, ORDER, 1)
    proj = dot_last(pair[...], grad_sin[0:ORDER, :])
    proj = proj[0:KROWS] + proj[48 : 48 + KROWS] + dot_last(pair[0:48, :], grad_sin[ORDER:, :])[0:KROWS]
    p_cos, p_sin = proj[0:BANDS], proj[BANDS : 2 * BANDS]
    p_lin, p_one = proj[2 * BANDS : 2 * BANDS + 1], proj[2 * BANDS + 1 : 2 * BANDS + 2]
    pay[...] = jnp.zeros((CTX * PIECE, LANES), f32)
    upper = lax.broadcasted_iota(jnp.int32, (CHAN, LANES), 1) >= ORDER
    pay[0:CHAN, :] = jnp.where(upper, second_part, 0.0)
    pay[CHAN : CHAN + 1, :] = skip_row
    pay[0:1, 0:ORDER] = (p_lin + start_frac * p_one) * freq_row
    pay[1 : 1 + BANDS, 0:ORDER] = (p_cos * cos_at - p_sin * sin_at) * freq_row
    pay[1 + BANDS : 1 + 2 * BANDS, 0:ORDER] = (p_cos * sin_at + p_sin * cos_at) * freq_row
    pay[33:34, 0:ORDER] = p_one * freq_row
    pay[34:35, 0:ORDER] = jnp.sum(proj * weights[...], axis=0, keepdims=True)

    for at in range(CTX):
        send_p[at] = pay[at * PIECE : (at + 1) * PIECE, :]
    send_all(send_p, recv_p, 4)

    wait_all(recv_f, 1)
    for at in range(N_ONE // chunk):
        rows = pl.ds(at * chunk, chunk)
        low_rows = pl.ds(N_ONE + at * chunk, chunk)
        cos_t, sin_t = turned(rows)
        filt_c = recv_f[...].reshape(N_ONE, LANES)
        a_real = dot(first[rows, :], filt_c)
        a_imag = dot(first[low_rows, :], filt_c)
        h_spec = spectrum(a_real, a_imag, cos_t, sin_t)
        h_r, h_i = h_spec[:, :LANES], h_spec[:, LANES:]
        w_r, w_i = spec_w[rows, 0:LANES], spec_w[rows, LANES : 2 * LANES]
        g_r, g_i = spec_g[rows, 0:LANES], spec_g[rows, LANES : 2 * LANES]
        d_real, d_imag = inverse_part(h_r * w_r - h_i * w_i, h_r * w_i + h_i * w_r, cos_t, sin_t)
        fold_b[rows, 0:LANES] = d_real
        fold_b[low_rows, 0:LANES] = d_imag
        d_real, d_imag = inverse_part(h_r * g_r + h_i * g_i, h_r * g_i - h_i * g_r, cos_t, sin_t)
        fold_b[rows, LANES : 2 * LANES] = d_real
        fold_b[low_rows, LANES : 2 * LANES] = d_imag
    spread = lax.broadcasted_iota(jnp.int32, (1, CHAN), 1)
    my_skip = jnp.sum(
        jnp.where(spread == me, skip_ref[...].reshape(1, CHAN), 0.0), axis=1, keepdims=True
    )
    direct = dot(first_t[...], fold_b[...]) + my_skip * both[...].astype(f32)
    send_mb[:, 0] = direct[:, :LANES].astype(bf16).reshape(CTX, ROWS, LANES)
    send_mb[:, 1] = direct[:, LANES:].astype(bf16).reshape(CTX, ROWS, LANES)


    wait_all(recv_p, 4)
    own = recv_p[0]
    for at in range(1, CTX):
        own = own + recv_p[at]
    piece[...] = own

    def send_slab(step, carry):
        peer = lax.rem(slab + step, SLAB)
        pltpu.make_async_remote_copy(
            src_ref=piece,
            dst_ref=recv_s.at[slab],
            send_sem=send_sem.at[5],
            recv_sem=recv_sem.at[5],
            device_id={"slab": peer},
            device_id_type=MESH,
        ).start()
        return carry

    lax.fori_loop(1, SLAB, send_slab, 0)
    pltpu.make_async_copy(piece, recv_s.at[slab], recv_sem.at[5]).start()
    send_all(send_mb, recv_mb, 3)

    wait_all(recv_s, 5)
    total = recv_s[0]
    for at in range(1, SLAB):
        total = total + recv_s[at]
    summed = lax.broadcasted_iota(jnp.int32, (PIECE, LANES), 1) < ORDER
    done[...] = jnp.where(summed, total, piece[...])

    def send_done(step, carry):
        peer = lax.rem(me + step, CTX)
        pltpu.make_async_remote_copy(
            src_ref=done,
            dst_ref=recv_d.at[me],
            send_sem=send_sem.at[6],
            recv_sem=recv_sem.at[6],
            device_id={"ctx": peer},
            device_id_type=MESH,
        ).start()
        return carry

    lax.fori_loop(1, CTX, send_done, 0)
    pltpu.make_async_copy(done, recv_d.at[me], recv_sem.at[6]).start()

    wait_all(recv_mb, 3)
    flat_a[...] = recv_mb[:, 0].astype(f32).reshape(N_ONE, LANES)
    flat_b[...] = recv_mb[:, 1].astype(f32).reshape(N_ONE, LANES)
    for col in range(ROWS):
        lanes = pl.ds(col * LANES, LANES)
        mid = flat_a[pl.ds(col, CHAN, stride=ROWS), :]
        back = flat_b[pl.ds(col, CHAN, stride=ROWS), :]
        query_out[:, lanes] = (grad_ref[:, lanes].astype(f32) * mid).astype(bf16)
        key_out[:, lanes] = (back * value_ref[:, lanes].astype(f32)).astype(bf16)
        value_out[:, lanes] = (back * key_ref[:, lanes].astype(f32)).astype(bf16)

    wait_sent(send_mg, CTX - 1, 0)
    wait_sent(send_f, CTX - 1, 1)
    wait_sent(send_gf, CTX - 1, 2)
    wait_sent(send_mb, CTX - 1, 3)
    wait_sent(send_p, CTX - 1, 4)
    wait_sent(recv_s, SLAB - 1, 5)
    wait_all(recv_d, 6)
    for at in range(CTX):
        sums_out[at * PIECE : (at + 1) * PIECE, :] = recv_d[at]
    wait_sent(recv_d, CTX - 1, 6)


def last_kernel(
    query_ref,
    key_ref,
    value_ref,
    sums_ref,
    query_out,
    key_out,
    value_out,
    first_out,
    bias_out,
    freq_out,
    second_out,
    skip_out,
    sem,
):
    stores = [
        pltpu.make_async_copy(source, target, sem.at[at])
        for at, (source, target) in enumerate(
            [(query_ref, query_out), (key_ref, key_out), (value_ref, value_out)]
        )
    ]
    for store in stores:
        store.start()
    first_out[...] = sums_ref[0:33, 0:ORDER]
    bias_out[...] = sums_ref[33:34, 0:ORDER].reshape(ORDER)
    freq_out[...] = sums_ref[34:35, 0:ORDER].reshape(ORDER)
    second_out[...] = sums_ref[0:CHAN, ORDER : 2 * ORDER]
    skip_out[...] = sums_ref[CHAN : CHAN + 1, ORDER : ORDER + CHAN].reshape(CHAN)
    for store in stores:
        store.wait()


def shards(
    query_in,
    key_in,
    value_in,
    grad_out,
    w_first,
    b_first,
    frequency,
    w_second,
    decay_rate,
    skip_gain,
):
    consts = tables()
    vmem = pl.BlockSpec(memory_space=pltpu.VMEM)
    hbm = pl.BlockSpec(memory_space=pltpu.HBM)
    block = lambda *dims: pltpu.VMEM(dims, bf16)
    wide = lambda *dims: pltpu.VMEM(dims, f32)
    blocks = (CTX, ROWS, LANES)
    pairs = (CTX, 2, ROWS, LANES)
    rows = jax.ShapeDtypeStruct((CHAN, PART), bf16)
    sums_shape = jax.ShapeDtypeStruct((CTX * PIECE, LANES), f32)
    query_g, key_g, value_g, sums = pl.pallas_call(
        main_kernel,
        name="hyena_backward",
        out_shape=(rows, rows, rows, sums_shape),
        in_specs=[hbm] * 18,
        out_specs=(vmem, vmem, vmem, vmem),
        scratch_shapes=[
            block(CHAN, PART),
            block(CHAN, PART),
            block(CHAN, PART),
            block(CHAN, PART),
            wide(33, ORDER),
            wide(ORDER),
            wide(ORDER),
            wide(CHAN, ORDER),
            wide(CHAN),
            wide(CHAN),
            block(2 * N_ONE, N_ONE),
            block(N_ONE, 2 * N_ONE),
            block(2 * LANES, 2 * LANES),
            block(2 * LANES, 2 * LANES),
            wide(N_ONE, 2 * LANES),
            block(6 * KROWS, PART),
            block(96, PART),
            wide(2, BANDS, LANES),
            wide(N_ONE, LANES),
            wide(N_ONE, LANES),
            block(*pairs),
            block(*pairs),
            block(*blocks),
            block(*blocks),
            block(*blocks),
            block(*blocks),
            block(*pairs),
            block(*pairs),
            wide(KROWS, ORDER),
            wide(6 * KROWS, ORDER),
            wide(ORDER, PART),
            block(2 * ORDER, PART),
            wide(ORDER, PART),
            wide(CHAN, PART),
            block(N_ONE, 2 * LANES),
            wide(N_ONE, 2 * LANES),
            wide(N_ONE, 2 * LANES),
            block(2 * N_ONE, LANES),
            block(2 * N_ONE, 2 * LANES),
            block(3 * CHAN, PART),
            block(2 * ORDER, PART),
            wide(CTX * PIECE, LANES),
            wide(CTX, PIECE, LANES),
            wide(CTX, PIECE, LANES),
            wide(PIECE, LANES),
            wide(SLAB, PIECE, LANES),
            wide(PIECE, LANES),
            wide(CTX, PIECE, LANES),
            pltpu.SemaphoreType.DMA((18,)),
            pltpu.SemaphoreType.DMA((7,)),
            pltpu.SemaphoreType.DMA((7,)),
        ],
        compiler_params=pltpu.CompilerParams(
            collective_id=0, has_side_effects=True, vmem_limit_bytes=40 * 1024 * 1024
        ),
    )(
        *[pltpu.with_memory_space_constraint(held, pltpu.HBM) for held in (
        query_in,
        key_in,
        value_in,
        grad_out,
        w_first,
        b_first,
        frequency,
        w_second.T,
        decay_rate,
        skip_gain,
        *consts,
        )]
    )
    vector = lambda count: jax.ShapeDtypeStruct((count,), f32)
    outs = pl.pallas_call(
        last_kernel,
        name="results",
        out_shape=(
            rows,
            rows,
            rows,
            jax.ShapeDtypeStruct((33, ORDER), f32),
            vector(ORDER),
            vector(ORDER),
            jax.ShapeDtypeStruct((CHAN, ORDER), f32),
            vector(CHAN),
        ),
        in_specs=[vmem] * 4,
        out_specs=(hbm, hbm, hbm, vmem, vmem, vmem, vmem, vmem),
        scratch_shapes=[pltpu.SemaphoreType.DMA((3,))],
        compiler_params=pltpu.CompilerParams(vmem_limit_bytes=56 * 1024 * 1024),
    )(*[pltpu.with_memory_space_constraint(held, pltpu.VMEM) for held in (query_g, key_g, value_g, sums)])
    return (*outs[:6], outs[6].T, outs[7])


def solution(mesh):
    placed = (
        P("slab", "ctx"),
        P("slab", "ctx"),
        P("slab", "ctx"),
        P("slab", "ctx"),
        P(),
        P(),
        P(),
        P(None, "slab"),
        P("slab"),
        P("slab"),
    )
    return jax.shard_map(
        shards,
        mesh=mesh,
        in_specs=placed,
        out_specs=(
            P("slab", "ctx"),
            P("slab", "ctx"),
            P("slab", "ctx"),
            P(),
            P(),
            P(),
            P(None, "slab"),
            P("slab"),
        ),
        check_vma=False,
    )
```

```python
import math

import jax
import jax.numpy as jnp
import ml_dtypes
import numpy as np
from jax import lax
from jax.experimental import pallas as pl
from jax.experimental.pallas import tpu as pltpu
from jax.sharding import PartitionSpec as P

BANDS = 16
CTX = 32
SLAB = 16
CHAN = 32
PART = 2048
SEQ = CTX * PART
ROWS = 16
LANES = 128
N_ONE = SEQ // LANES
ORDER = 64
KROWS = 40
Z_LO, Z_HI, Y_ALL, FLAT = 4, 4, 4, 8
PLANE = Y_ALL * FLAT
Z_ALL = Z_HI * Z_LO

MESH = pl.DeviceIdType.MESH
f32, bf16 = jnp.float32, jnp.bfloat16


def np_parts(table, count):
    out, rest = [], np.asarray(table, np.float64)
    for _ in range(count):
        part = rest.astype(np.float32).astype(ml_dtypes.bfloat16)
        out.append(part)
        rest = rest - part.astype(np.float64)
    return out


def tables():
    k_one = np.arange(N_ONE)[:, None]
    n_one = np.arange(N_ONE)[None, :]
    phase = 2 * np.pi * (((4 * k_one + 1) * n_one) % (4 * N_ONE)) / (4 * N_ONE)
    first = np.concatenate([np.cos(phase), -np.sin(phase)], axis=0)
    n_two = np.arange(LANES)[None, :]
    turn = 2 * np.pi * (k_one + 0.25) * n_two / SEQ
    twiddle = np.concatenate([np.cos(turn), np.sin(turn)], axis=1).astype(np.float32)
    small = 2 * np.pi * ((np.arange(LANES)[:, None] * n_two) % LANES) / LANES
    cos_s, sin_s = np.cos(small), np.sin(small)
    second = np.block([[cos_s, -sin_s], [sin_s, cos_s]])
    second_inv = np.block([[cos_s, sin_s], [-sin_s, cos_s]])
    place = np.arange(PART)
    bands = np.arange(1, BANDS + 1)
    arc = 2 * np.pi * (bands[:, None] * place[None, :] % SEQ) / SEQ
    base = np.zeros((KROWS, PART))
    base[:BANDS], base[BANDS : 2 * BANDS] = np.cos(arc), np.sin(arc)
    base[2 * BANDS], base[2 * BANDS + 1] = place / SEQ, 1.0
    b_one, b_two, b_three = np_parts(base, 3)
    stacked = np.concatenate([b_one, b_two, b_one, b_three, b_two, b_one], axis=0)
    pair = np.zeros((96, PART), ml_dtypes.bfloat16)
    pair[:KROWS], pair[48 : 48 + KROWS] = b_one, b_two
    start = 2 * np.pi * (bands[None, :] * np.arange(CTX)[:, None] % CTX) / CTX
    rot = np.stack([np.cos(start), np.sin(start)], axis=1).astype(np.float32)
    rot = np.broadcast_to(rot[:, :, :, None], (CTX, 2, BANDS, LANES)).copy()
    one = lambda table: np_parts(table, 1)[0]
    return (
        one(first),
        one(first.T / SEQ),
        one(second),
        one(second_inv),
        twiddle,
        stacked,
        pair,
        rot,
    )


def dot(left, right):
    return jnp.dot(left, right, preferred_element_type=f32)


def dot_first(left, right):
    return lax.dot_general(left, right, (((0,), (0,)), ((), ())), preferred_element_type=f32)


def dot_last(left, right):
    return lax.dot_general(left, right, (((1,), (1,)), ((), ())), preferred_element_type=f32)


def high_low(value):
    high = value.astype(bf16)
    return high, (value - high.astype(f32)).astype(bf16)


def eye(count):
    rows = lax.broadcasted_iota(jnp.int32, (count, count), 0)
    return rows == lax.broadcasted_iota(jnp.int32, (count, count), 1)


def as_column(row, count):
    spread = jnp.broadcast_to(row, (count, count))
    return jnp.sum(jnp.where(eye(count), spread, 0.0), axis=1, keepdims=True)


def as_row(column, count):
    spread = jnp.broadcast_to(column, (count, count))
    return jnp.sum(jnp.where(eye(count), spread, 0.0), axis=0, keepdims=True)


def sine_cosine(quarters):
    whole = jnp.floor(quarters + 0.5)
    rest = quarters - whole
    turn = whole.astype(jnp.int32)
    angle = rest * (math.pi / 2)
    square = angle * angle
    sine = angle + angle * square * (
        -1.0 / 6 + square * (1.0 / 120 + square * (-1.0 / 5040 + square * (1.0 / 362880)))
    )
    cosine = 1.0 + square * (
        -0.5 + square * (1.0 / 24 + square * (-1.0 / 720 + square * (1.0 / 40320)))
    )
    swap = (turn & 1) == 1
    sin_val = jnp.where(swap, cosine, sine)
    cos_val = jnp.where(swap, sine, cosine)
    sin_val = jnp.where((turn & 2) == 2, -sin_val, sin_val)
    cos_val = jnp.where(((turn + 1) & 2) == 2, -cos_val, cos_val)
    return sin_val, cos_val


def main_kernel(
    query_hbm,
    key_hbm,
    value_hbm,
    grad_hbm,
    w_first_hbm,
    b_first_hbm,
    freq_hbm,
    w_second_hbm,
    decay_hbm,
    skip_hbm,
    first_hbm,
    first_t_hbm,
    second_hbm,
    second_inv_hbm,
    twiddle_hbm,
    stacked_hbm,
    pair_hbm,
    rot_hbm,
    query_out,
    key_out,
    value_out,
    sums_out,
    query_ref,
    key_ref,
    value_ref,
    grad_ref,
    w_first_ref,
    b_first_ref,
    freq_ref,
    w_second_ref,
    decay_ref,
    skip_ref,
    first,
    first_t,
    second,
    second_inv,
    twiddle,
    stacked,
    pair,
    rot,
    flat_a,
    flat_b,
    send_mg,
    recv_mg,
    send_f,
    recv_f,
    send_gf,
    recv_gf,
    send_mb,
    recv_mb,
    weights,
    weight_stack,
    quarters,
    hidden,
    cosines,
    modul,
    both,
    spec_w,
    spec_g,
    fold_a,
    fold_b,
    grad_mod,
    grad_sin,
    spare,
    pay,
    recv_p,
    piece,
    recv_s,
    done,
    recv_d,
    pay_own,
    recv_own,
    done_own,
    all_own,
    table_sem,
    send_sem,
    recv_sem,
    entered,
):
    me = lax.axis_index("ctx")
    slab = lax.axis_index("slab")

    barrier = pltpu.get_barrier_semaphore()

    def greet_ctx(step, carry):
        pl.semaphore_signal(
            barrier, inc=1, device_id={"ctx": lax.rem(me + step, CTX)}, device_id_type=MESH
        )
        return carry

    zl, flat = lax.div(me, FLAT), lax.rem(me, FLAT)
    zh, yy = lax.div(slab, Y_ALL), lax.rem(slab, Y_ALL)
    depth = zh * Z_LO + zl
    at_plane = yy * FLAT + flat

    def in_plane(at):
        return {
            "ctx": zl * FLAT + lax.rem(at, FLAT),
            "slab": zh * Y_ALL + lax.div(at, FLAT),
        }

    def in_column(at):
        return {
            "ctx": lax.rem(at, Z_LO) * FLAT + flat,
            "slab": lax.div(at, Z_LO) * Y_ALL + yy,
        }

    def signal_each(semaphore, place, first_at, last_at):
        def body(at, carry):
            pl.semaphore_signal(semaphore, inc=1, device_id=place(at), device_id_type=MESH)
            return carry

        lax.fori_loop(first_at, last_at, body, 0)

    lax.fori_loop(1, CTX, greet_ctx, 0)
    signal_each(barrier, in_plane, (yy + 1) * FLAT, PLANE)
    signal_each(barrier, in_column, (zh + 1) * Z_LO, Z_ALL)

    def load(source, target, at):
        copy = pltpu.make_async_copy(source, target, table_sem.at[at])
        copy.start()
        return copy

    gates = [
        load(source, target, at)
        for at, (source, target) in enumerate(
            [(key_hbm, key_ref), (value_hbm, value_ref), (grad_hbm, grad_ref), (query_hbm, query_ref)]
        )
    ]
    layers = [
        load(source, target, 4 + at)
        for at, (source, target) in enumerate(
            [
                (rot_hbm.at[me], rot),
                (w_first_hbm, w_first_ref),
                (b_first_hbm, b_first_ref),
                (freq_hbm, freq_ref),
                (w_second_hbm, w_second_ref),
                (decay_hbm, decay_ref),
                (skip_hbm, skip_ref),
                (stacked_hbm, stacked),
            ]
        )
    ]
    transforms = [
        load(source, target, 12 + at)
        for at, (source, target) in enumerate(
            [
                (first_hbm, first),
                (second_hbm, second),
                (second_inv_hbm, second_inv),
                (twiddle_hbm, twiddle),
                (first_t_hbm, first_t),
                (pair_hbm, pair),
            ]
        )
    ]

    def wait_loads(copies):
        for copy in copies:
            copy.wait()

    def send_all(source, target, at):
        def body(step, carry):
            peer = lax.rem(me + step, CTX)
            pltpu.make_async_remote_copy(
                src_ref=source.at[peer],
                dst_ref=target.at[me],
                send_sem=send_sem.at[at],
                recv_sem=recv_sem.at[at],
                device_id={"ctx": peer},
                device_id_type=MESH,
            ).start()
            return carry

        lax.fori_loop(1, CTX, body, 0)
        pltpu.make_async_copy(source.at[me], target.at[me], recv_sem.at[at]).start()

    def wait_all(target, at):
        pltpu.make_async_copy(target, target, recv_sem.at[at]).wait()

    def wait_sent(source, count, at):
        part = source.at[pl.ds(0, count)]
        pltpu.make_async_copy(part, part, send_sem.at[at]).wait()

    wait_loads(gates)
    skip_acc = jnp.zeros((CHAN, LANES), f32)
    for col in range(ROWS):
        lanes = pl.ds(col * LANES, LANES)
        mixed = key_ref[:, lanes].astype(f32) * value_ref[:, lanes].astype(f32)
        mixed = mixed.astype(bf16).astype(f32)
        mid = grad_ref[:, lanes].astype(f32) * query_ref[:, lanes].astype(f32)
        mid = mid.astype(bf16).astype(f32)
        flat_a[pl.ds(col, CHAN, stride=ROWS), :] = mixed
        flat_b[pl.ds(col, CHAN, stride=ROWS), :] = mid
        skip_acc = skip_acc + mixed * mid
    send_mg[:, 0] = flat_a[...].reshape(CHAN, ROWS, LANES).astype(bf16)
    send_mg[:, 1] = flat_b[...].reshape(CHAN, ROWS, LANES).astype(bf16)
    skip_sum = jnp.sum(skip_acc, axis=1, keepdims=True)

    wait_loads(layers)
    cos_at, sin_at = rot[0][:, :ORDER], rot[1][:, :ORDER]
    w_lin = w_first_ref[0:1, :]
    w_cos = w_first_ref[1 : 1 + BANDS, :]
    w_sin = w_first_ref[1 + BANDS : 1 + 2 * BANDS, :]
    start_frac = me.astype(f32) * (1.0 / CTX)
    weights[...] = jnp.zeros((KROWS, ORDER), f32)
    weights[0:BANDS, :] = w_cos * cos_at + w_sin * sin_at
    weights[BANDS : 2 * BANDS, :] = w_sin * cos_at - w_cos * sin_at
    weights[2 * BANDS : 2 * BANDS + 1, :] = w_lin
    freq_row = freq_ref[...].reshape(1, ORDER)
    weights[2 * BANDS + 1 : 2 * BANDS + 2, :] = (
        b_first_ref[...].reshape(1, ORDER) + w_lin * start_frac
    )
    scaled = weights[...] * (freq_row * (2.0 / math.pi))
    part_one = scaled.astype(bf16).astype(f32)
    rest = scaled - part_one
    part_two = rest.astype(bf16).astype(f32)
    part_three = (rest - part_two).astype(bf16).astype(f32)
    for at, part in enumerate([part_one, part_one, part_two, part_one, part_two, part_three]):
        weight_stack[at * KROWS : (at + 1) * KROWS, :] = part
    quarters[...] = dot_first(weight_stack[...].astype(bf16), stacked[...])
    decay_col = as_column(decay_ref[...].reshape(1, CHAN), CHAN)
    small = -2.0 * decay_col
    grown = small * (
        1.0 + small / 2 * (1.0 + small / 3 * (1.0 + small / 4 * (1.0 + small / 5 * (1.0 + small / 6))))
    )
    scaling = jnp.sqrt(grown / (jnp.exp(small * SEQ) - 1.0))
    wide = 256
    for col in range(PART // wide):
        lanes = pl.ds(col * wide, wide)
        sin_val, cos_val = sine_cosine(quarters[:, lanes])
        high, low = high_low(sin_val)
        hidden[0:ORDER, lanes] = high
        hidden[ORDER : 2 * ORDER, lanes] = low
        cosines[:, lanes] = cos_val
        times = lax.broadcasted_iota(jnp.int32, (CHAN, wide), 1) + (me * PART + col * wide)
        modul[:, lanes] = jnp.exp(-decay_col * times.astype(f32)) * scaling
    w_high, w_low = high_low(w_second_ref[...])
    filt = dot(jnp.concatenate([w_high, w_low], axis=0), hidden[0:ORDER, :])
    filt = filt[:CHAN] + filt[CHAN:] + dot(w_high, hidden[ORDER : 2 * ORDER, :])
    filt = filt * modul[...]
    for col in range(ROWS):
        flat_a[pl.ds(col, CHAN, stride=ROWS), :] = filt[:, col * LANES : (col + 1) * LANES]
    send_f[...] = flat_a[...].reshape(CHAN, ROWS, LANES).astype(bf16)

    pl.semaphore_wait(barrier, CTX - 1 + yy * FLAT + zh * Z_LO)
    send_all(send_mg, recv_mg, 0)
    signal_each(entered, in_plane, 0, yy * FLAT)
    signal_each(entered, in_column, 0, zh * Z_LO)

    wait_loads(transforms)
    wait_all(recv_mg, 0)
    both[:, 0:LANES] = recv_mg[:, 0].reshape(N_ONE, LANES)
    both[:, LANES : 2 * LANES] = recv_mg[:, 1].reshape(N_ONE, LANES)
    chunk = 256

    def turned(rows):
        return twiddle[rows, 0:LANES], twiddle[rows, LANES : 2 * LANES]

    def inverse_part(real, imag, cos_t, sin_t):
        back = dot(jnp.concatenate([real, imag], axis=1).astype(bf16), second_inv[...])
        c_real, c_imag = back[:, :LANES], back[:, LANES:]
        return (
            (c_real * cos_t - c_imag * sin_t).astype(bf16),
            (c_imag * cos_t + c_real * sin_t).astype(bf16),
        )

    def spectrum(a_real, a_imag, cos_t, sin_t):
        b_real = a_real * cos_t + a_imag * sin_t
        b_imag = a_imag * cos_t - a_real * sin_t
        return dot(jnp.concatenate([b_real, b_imag], axis=1).astype(bf16), second[...])

    for at in range(N_ONE // chunk):
        rows = pl.ds(at * chunk, chunk)
        low_rows = pl.ds(N_ONE + at * chunk, chunk)
        cos_t, sin_t = turned(rows)
        a_real = dot(first[rows, :], both[...])
        a_imag = dot(first[low_rows, :], both[...])
        w_spec = spectrum(a_real[:, :LANES], a_imag[:, :LANES], cos_t, sin_t)
        g_spec = spectrum(a_real[:, LANES:], a_imag[:, LANES:], cos_t, sin_t)
        spec_w[rows, :] = w_spec
        spec_g[rows, :] = g_spec
        w_r, w_i, g_r, g_i = w_spec[:, :LANES], w_spec[:, LANES:], g_spec[:, :LANES], g_spec[:, LANES:]
        d_real, d_imag = inverse_part(w_r * g_r + w_i * g_i, w_r * g_i - w_i * g_r, cos_t, sin_t)
        fold_a[rows, :] = d_real
        fold_a[low_rows, :] = d_imag
    send_gf[...] = dot(first_t[...], fold_a[...]).astype(bf16).reshape(CTX, ROWS, LANES)
    send_all(send_gf, recv_gf, 2)

    wait_all(recv_gf, 2)
    flat_a[...] = recv_gf[...].astype(f32).reshape(N_ONE, LANES)
    for col in range(ROWS):
        lanes = pl.ds(col * LANES, LANES)
        part = flat_a[pl.ds(col, CHAN, stride=ROWS), :] * modul[:, lanes]
        high, low = high_low(part)
        grad_mod[0:CHAN, lanes] = high
        grad_mod[CHAN : 2 * CHAN, lanes] = low
        grad_mod[2 * CHAN : 3 * CHAN, lanes] = high
    grad_hidden = dot_first(jnp.concatenate([w_high, w_high, w_low], axis=0), grad_mod[...])
    high, low = high_low(grad_hidden * cosines[...])
    grad_sin[0:ORDER, :] = high
    grad_sin[ORDER : 2 * ORDER, :] = low
    second_part = dot_last(grad_mod[0 : 2 * CHAN, :], hidden[...])
    high_part = second_part[:CHAN]
    low_part = jnp.where(
        lax.broadcasted_iota(jnp.int32, (CHAN, LANES), 1) < ORDER, second_part[CHAN:], 0.0
    )
    second_part = high_part + low_part
    second_part = second_part + pltpu.roll(second_part, ORDER, 1)
    proj = dot_last(pair[...], grad_sin[0:ORDER, :])
    proj = proj[0:KROWS] + proj[48 : 48 + KROWS] + dot_last(pair[0:48, :], grad_sin[ORDER:, :])[0:KROWS]
    p_cos, p_sin = proj[0:BANDS], proj[BANDS : 2 * BANDS]
    p_lin, p_one = proj[2 * BANDS : 2 * BANDS + 1], proj[2 * BANDS + 1 : 2 * BANDS + 2]
    grad_first_rows = jnp.concatenate(
        [
            (p_cos * cos_at - p_sin * sin_at) * freq_row,
            (p_cos * sin_at + p_sin * cos_at) * freq_row,
        ],
        axis=0,
    )
    spare[...] = jnp.zeros((8, LANES), f32)
    spare[0:1, 0:ORDER] = (p_lin + start_frac * p_one) * freq_row
    spare[1:2, 0:ORDER] = p_one * freq_row
    spare[2:3, 0:ORDER] = jnp.sum(proj * weights[...], axis=0, keepdims=True)
    moved = pltpu.roll(spare[...], ORDER, 1)
    for at in range(PLANE):
        pay[at, :, 0:ORDER] = grad_first_rows[at : at + 1, :]
        pay[at, :, ORDER:LANES] = (
            moved[at : at + 1, ORDER:LANES] if at < 3 else jnp.zeros((1, ORDER), f32)
        )

    def send_each(source, target, slot, at, place, own, count, fixed):
        def body(step, carry):
            peer = lax.rem(own + step, count)
            pltpu.make_async_remote_copy(
                src_ref=source if fixed else source.at[peer],
                dst_ref=target.at[slot],
                send_sem=send_sem.at[at],
                recv_sem=recv_sem.at[at],
                device_id=place(peer),
                device_id_type=MESH,
            ).start()
            return carry

        lax.fori_loop(1, count, body, 0)
        pltpu.make_async_copy(
            source if fixed else source.at[own], target.at[slot], recv_sem.at[at]
        ).start()

    def in_ctx(at):
        return {"ctx": at}

    above = (Y_ALL - 1 - yy) * FLAT + (Z_HI - 1 - zh) * Z_LO

    @pl.when(above > 0)
    def _():
        pl.semaphore_wait(entered, above)

    send_each(pay, recv_p, at_plane, 4, in_plane, at_plane, PLANE, False)
    for at in range(CTX):
        pay_own[at] = jnp.where(
            lax.broadcasted_iota(jnp.int32, (1, LANES), 1) < ORDER,
            second_part[at : at + 1, :],
            jnp.broadcast_to(skip_sum[at : at + 1, :], (1, LANES)),
        )
    send_each(pay_own, recv_own, me, 7, in_ctx, me, CTX, False)
    send_all(send_f, recv_f, 1)

    def add_up(ref, count):
        total = ref[0]
        for at in range(1, count):
            total = total + ref[at]
        return total

    wait_all(recv_p, 4)
    piece[...] = add_up(recv_p, PLANE)
    send_each(piece, recv_s, depth, 5, in_column, depth, Z_ALL, True)
    wait_all(recv_own, 7)
    done_own[...] = add_up(recv_own, CTX)
    send_each(done_own, all_own, me, 8, in_ctx, me, CTX, True)

    wait_all(recv_f, 1)
    for at in range(N_ONE // chunk):
        rows = pl.ds(at * chunk, chunk)
        low_rows = pl.ds(N_ONE + at * chunk, chunk)
        cos_t, sin_t = turned(rows)
        filt_c = recv_f[...].reshape(N_ONE, LANES)
        a_real = dot(first[rows, :], filt_c)
        a_imag = dot(first[low_rows, :], filt_c)
        h_spec = spectrum(a_real, a_imag, cos_t, sin_t)
        h_r, h_i = h_spec[:, :LANES], h_spec[:, LANES:]
        w_r, w_i = spec_w[rows, 0:LANES], spec_w[rows, LANES : 2 * LANES]
        g_r, g_i = spec_g[rows, 0:LANES], spec_g[rows, LANES : 2 * LANES]
        d_real, d_imag = inverse_part(h_r * w_r - h_i * w_i, h_r * w_i + h_i * w_r, cos_t, sin_t)
        fold_b[rows, 0:LANES] = d_real
        fold_b[low_rows, 0:LANES] = d_imag
        d_real, d_imag = inverse_part(h_r * g_r + h_i * g_i, h_r * g_i - h_i * g_r, cos_t, sin_t)
        fold_b[rows, LANES : 2 * LANES] = d_real
        fold_b[low_rows, LANES : 2 * LANES] = d_imag
    spread = lax.broadcasted_iota(jnp.int32, (1, CHAN), 1)
    my_skip = jnp.sum(
        jnp.where(spread == me, skip_ref[...].reshape(1, CHAN), 0.0), axis=1, keepdims=True
    )
    direct = dot(first_t[...], fold_b[...]) + my_skip * both[...].astype(f32)
    send_mb[:, 0] = direct[:, :LANES].astype(bf16).reshape(CTX, ROWS, LANES)
    send_mb[:, 1] = direct[:, LANES:].astype(bf16).reshape(CTX, ROWS, LANES)


    send_all(send_mb, recv_mb, 3)

    wait_all(recv_s, 5)
    done[...] = add_up(recv_s, Z_ALL)
    send_each(done, recv_d, at_plane, 6, in_plane, at_plane, PLANE, True)

    wait_all(recv_mb, 3)
    flat_a[...] = recv_mb[:, 0].astype(f32).reshape(N_ONE, LANES)
    flat_b[...] = recv_mb[:, 1].astype(f32).reshape(N_ONE, LANES)
    for col in range(ROWS):
        lanes = pl.ds(col * LANES, LANES)
        mid = flat_a[pl.ds(col, CHAN, stride=ROWS), :]
        back = flat_b[pl.ds(col, CHAN, stride=ROWS), :]
        query_out[:, lanes] = (grad_ref[:, lanes].astype(f32) * mid).astype(bf16)
        key_out[:, lanes] = (back * value_ref[:, lanes].astype(f32)).astype(bf16)
        value_out[:, lanes] = (back * key_ref[:, lanes].astype(f32)).astype(bf16)

    wait_sent(send_mg, CTX - 1, 0)
    wait_sent(send_f, CTX - 1, 1)
    wait_sent(send_gf, CTX - 1, 2)
    wait_sent(send_mb, CTX - 1, 3)
    wait_sent(pay, PLANE - 1, 4)
    wait_sent(recv_s, Z_ALL - 1, 5)
    wait_sent(pay_own, CTX - 1, 7)
    wait_sent(all_own, CTX - 1, 8)
    wait_all(all_own, 8)
    for at in range(CTX):
        sums_out[PLANE + at : PLANE + at + 1, :] = all_own[at]
    wait_all(recv_d, 6)
    for at in range(PLANE):
        sums_out[at : at + 1, :] = recv_d[at]
    wait_sent(recv_d, PLANE - 1, 6)


def last_kernel(
    query_ref,
    key_ref,
    value_ref,
    sums_ref,
    query_out,
    key_out,
    value_out,
    first_out,
    bias_out,
    freq_out,
    second_out,
    skip_out,
    sem,
):
    stores = [
        pltpu.make_async_copy(source, target, sem.at[at])
        for at, (source, target) in enumerate(
            [(query_ref, query_out), (key_ref, key_out), (value_ref, value_out)]
        )
    ]
    for store in stores:
        store.start()
    first_out[1 : 1 + 2 * BANDS, :] = sums_ref[0 : 2 * BANDS, 0:ORDER]
    upper = pltpu.roll(sums_ref[0:8, :], ORDER, 1)
    first_out[0:1, :] = upper[0:1, 0:ORDER]
    bias_out[...] = upper[1:2, 0:ORDER].reshape(ORDER)
    freq_out[...] = upper[2:3, 0:ORDER].reshape(ORDER)
    second_out[...] = sums_ref[PLANE : PLANE + CHAN, 0:ORDER]
    skip_row = as_row(sums_ref[PLANE : PLANE + CHAN, ORDER : ORDER + 1], CHAN)
    skip_out[...] = skip_row.reshape(CHAN)
    for store in stores:
        store.wait()


def shards(
    query_in,
    key_in,
    value_in,
    grad_out,
    w_first,
    b_first,
    frequency,
    w_second,
    decay_rate,
    skip_gain,
):
    consts = tables()
    vmem = pl.BlockSpec(memory_space=pltpu.VMEM)
    hbm = pl.BlockSpec(memory_space=pltpu.HBM)
    block = lambda *dims: pltpu.VMEM(dims, bf16)
    wide = lambda *dims: pltpu.VMEM(dims, f32)
    blocks = (CTX, ROWS, LANES)
    pairs = (CTX, 2, ROWS, LANES)
    rows = jax.ShapeDtypeStruct((CHAN, PART), bf16)
    sums_shape = jax.ShapeDtypeStruct((PLANE + CTX, LANES), f32)
    query_g, key_g, value_g, sums = pl.pallas_call(
        main_kernel,
        name="hyena_backward",
        out_shape=(rows, rows, rows, sums_shape),
        in_specs=[hbm] * 18,
        out_specs=(vmem, vmem, vmem, vmem),
        scratch_shapes=[
            block(CHAN, PART),
            block(CHAN, PART),
            block(CHAN, PART),
            block(CHAN, PART),
            wide(33, ORDER),
            wide(ORDER),
            wide(ORDER),
            wide(CHAN, ORDER),
            wide(CHAN),
            wide(CHAN),
            block(2 * N_ONE, N_ONE),
            block(N_ONE, 2 * N_ONE),
            block(2 * LANES, 2 * LANES),
            block(2 * LANES, 2 * LANES),
            wide(N_ONE, 2 * LANES),
            block(6 * KROWS, PART),
            block(96, PART),
            wide(2, BANDS, LANES),
            wide(N_ONE, LANES),
            wide(N_ONE, LANES),
            block(*pairs),
            block(*pairs),
            block(*blocks),
            block(*blocks),
            block(*blocks),
            block(*blocks),
            block(*pairs),
            block(*pairs),
            wide(KROWS, ORDER),
            wide(6 * KROWS, ORDER),
            wide(ORDER, PART),
            block(2 * ORDER, PART),
            wide(ORDER, PART),
            wide(CHAN, PART),
            block(N_ONE, 2 * LANES),
            wide(N_ONE, 2 * LANES),
            wide(N_ONE, 2 * LANES),
            block(2 * N_ONE, LANES),
            block(2 * N_ONE, 2 * LANES),
            block(3 * CHAN, PART),
            block(2 * ORDER, PART),
            wide(8, LANES),
            wide(PLANE, 1, LANES),
            wide(PLANE, 1, LANES),
            wide(1, LANES),
            wide(Z_ALL, 1, LANES),
            wide(1, LANES),
            wide(PLANE, 1, LANES),
            wide(CTX, 1, LANES),
            wide(CTX, 1, LANES),
            wide(1, LANES),
            wide(CTX, 1, LANES),
            pltpu.SemaphoreType.DMA((18,)),
            pltpu.SemaphoreType.DMA((9,)),
            pltpu.SemaphoreType.DMA((9,)),
            pltpu.SemaphoreType.REGULAR,
        ],
        compiler_params=pltpu.CompilerParams(
            collective_id=0, has_side_effects=True, vmem_limit_bytes=40 * 1024 * 1024
        ),
    )(
        *[pltpu.with_memory_space_constraint(held, pltpu.HBM) for held in (
        query_in,
        key_in,
        value_in,
        grad_out,
        w_first,
        b_first,
        frequency,
        w_second.T,
        decay_rate,
        skip_gain,
        *consts,
        )]
    )
    vector = lambda count: jax.ShapeDtypeStruct((count,), f32)
    outs = pl.pallas_call(
        last_kernel,
        name="results",
        out_shape=(
            rows,
            rows,
            rows,
            jax.ShapeDtypeStruct((33, ORDER), f32),
            vector(ORDER),
            vector(ORDER),
            jax.ShapeDtypeStruct((CHAN, ORDER), f32),
            vector(CHAN),
        ),
        in_specs=[vmem] * 4,
        out_specs=(hbm, hbm, hbm, vmem, vmem, vmem, vmem, vmem),
        scratch_shapes=[pltpu.SemaphoreType.DMA((3,))],
        compiler_params=pltpu.CompilerParams(vmem_limit_bytes=56 * 1024 * 1024),
    )(*[pltpu.with_memory_space_constraint(held, pltpu.VMEM) for held in (query_g, key_g, value_g, sums)])
    return (*outs[:6], outs[6].T, outs[7])


def solution(mesh):
    placed = (
        P("slab", "ctx"),
        P("slab", "ctx"),
        P("slab", "ctx"),
        P("slab", "ctx"),
        P(),
        P(),
        P(),
        P(None, "slab"),
        P("slab"),
        P("slab"),
    )
    return jax.shard_map(
        shards,
        mesh=mesh,
        in_specs=placed,
        out_specs=(
            P("slab", "ctx"),
            P("slab", "ctx"),
            P("slab", "ctx"),
            P(),
            P(),
            P(),
            P(None, "slab"),
            P("slab"),
        ),
        check_vma=False,
    )
```

```python
import math

import jax
import jax.numpy as jnp
import ml_dtypes
import numpy as np
from jax import lax
from jax.experimental import pallas as pl
from jax.experimental.pallas import tpu as pltpu
from jax.sharding import PartitionSpec as P

BANDS = 16
CTX = 32
SLAB = 16
CHAN = 32
PART = 2048
SEQ = CTX * PART
ROWS = 16
LANES = 128
N_ONE = SEQ // LANES
ORDER = 64
KROWS = 40
Z_LO, Z_HI, Y_ALL, FLAT = 4, 4, 4, 8
PLANE = Y_ALL * FLAT
Z_ALL = Z_HI * Z_LO

MESH = pl.DeviceIdType.MESH
f32, bf16 = jnp.float32, jnp.bfloat16


def np_parts(table, count):
    out, rest = [], np.asarray(table, np.float64)
    for _ in range(count):
        part = rest.astype(np.float32).astype(ml_dtypes.bfloat16)
        out.append(part)
        rest = rest - part.astype(np.float64)
    return out


def tables():
    k_one = np.arange(N_ONE)[:, None]
    n_one = np.arange(N_ONE)[None, :]
    phase = 2 * np.pi * (((4 * k_one + 1) * n_one) % (4 * N_ONE)) / (4 * N_ONE)
    first = np.concatenate([np.cos(phase), -np.sin(phase)], axis=0)
    n_two = np.arange(LANES)[None, :]
    turn = 2 * np.pi * (k_one + 0.25) * n_two / SEQ
    twiddle = np.concatenate([np.cos(turn), np.sin(turn)], axis=1).astype(np.float32)
    small = 2 * np.pi * ((np.arange(LANES)[:, None] * n_two) % LANES) / LANES
    cos_s, sin_s = np.cos(small), np.sin(small)
    second = np.block([[cos_s, -sin_s], [sin_s, cos_s]])
    second_inv = np.block([[cos_s, sin_s], [-sin_s, cos_s]])
    place = np.arange(PART)
    bands = np.arange(1, BANDS + 1)
    arc = 2 * np.pi * (bands[:, None] * place[None, :] % SEQ) / SEQ
    base = np.zeros((KROWS, PART))
    base[:BANDS], base[BANDS : 2 * BANDS] = np.cos(arc), np.sin(arc)
    base[2 * BANDS], base[2 * BANDS + 1] = place / SEQ, 1.0
    b_one, b_two, b_three = np_parts(base, 3)
    stacked = np.concatenate([b_one, b_two, b_one, b_three, b_two, b_one], axis=0)
    pair = np.zeros((96, PART), ml_dtypes.bfloat16)
    pair[:KROWS], pair[48 : 48 + KROWS] = b_one, b_two
    start = 2 * np.pi * (bands[None, :] * np.arange(CTX)[:, None] % CTX) / CTX
    rot = np.stack([np.cos(start), np.sin(start)], axis=1).astype(np.float32)
    rot = np.broadcast_to(rot[:, :, :, None], (CTX, 2, BANDS, LANES)).copy()
    one = lambda table: np_parts(table, 1)[0]
    return (
        one(first),
        one(first.T / SEQ),
        one(second),
        one(second_inv),
        twiddle,
        stacked,
        pair,
        rot,
    )


def dot(left, right):
    return jnp.dot(left, right, preferred_element_type=f32)


def dot_first(left, right):
    return lax.dot_general(left, right, (((0,), (0,)), ((), ())), preferred_element_type=f32)


def dot_last(left, right):
    return lax.dot_general(left, right, (((1,), (1,)), ((), ())), preferred_element_type=f32)


def high_low(value):
    high = value.astype(bf16)
    return high, (value - high.astype(f32)).astype(bf16)


def eye(count):
    rows = lax.broadcasted_iota(jnp.int32, (count, count), 0)
    return rows == lax.broadcasted_iota(jnp.int32, (count, count), 1)


def as_column(row, count):
    spread = jnp.broadcast_to(row, (count, count))
    return jnp.sum(jnp.where(eye(count), spread, 0.0), axis=1, keepdims=True)


def as_row(column, count):
    spread = jnp.broadcast_to(column, (count, count))
    return jnp.sum(jnp.where(eye(count), spread, 0.0), axis=0, keepdims=True)


def sine_cosine(quarters):
    whole = jnp.floor(quarters + 0.5)
    rest = quarters - whole
    turn = whole.astype(jnp.int32)
    angle = rest * (math.pi / 2)
    square = angle * angle
    sine = angle + angle * square * (
        -1.0 / 6 + square * (1.0 / 120 + square * (-1.0 / 5040 + square * (1.0 / 362880)))
    )
    cosine = 1.0 + square * (
        -0.5 + square * (1.0 / 24 + square * (-1.0 / 720 + square * (1.0 / 40320)))
    )
    swap = (turn & 1) == 1
    sin_val = jnp.where(swap, cosine, sine)
    cos_val = jnp.where(swap, sine, cosine)
    sin_val = jnp.where((turn & 2) == 2, -sin_val, sin_val)
    cos_val = jnp.where(((turn + 1) & 2) == 2, -cos_val, cos_val)
    return sin_val, cos_val


def main_kernel(
    query_hbm,
    key_hbm,
    value_hbm,
    grad_hbm,
    w_first_hbm,
    b_first_hbm,
    freq_hbm,
    w_second_hbm,
    decay_hbm,
    skip_hbm,
    first_hbm,
    first_t_hbm,
    second_hbm,
    second_inv_hbm,
    twiddle_hbm,
    stacked_hbm,
    pair_hbm,
    rot_hbm,
    query_out,
    key_out,
    value_out,
    sums_out,
    query_ref,
    key_ref,
    value_ref,
    grad_ref,
    w_first_ref,
    b_first_ref,
    freq_ref,
    w_second_ref,
    decay_ref,
    skip_ref,
    first,
    first_t,
    second,
    second_inv,
    twiddle,
    stacked,
    pair,
    rot,
    flat_a,
    flat_b,
    send_mg,
    recv_mg,
    send_f,
    recv_f,
    send_gf,
    recv_gf,
    send_mb,
    recv_mb,
    weights,
    weight_stack,
    quarters,
    hidden,
    cosines,
    modul,
    both,
    spec_w,
    spec_g,
    fold_a,
    fold_b,
    grad_mod,
    grad_sin,
    spare,
    pay,
    recv_p,
    piece,
    recv_s,
    done,
    recv_d,
    pay_own,
    recv_own,
    done_own,
    all_own,
    table_sem,
    send_sem,
    recv_sem,
    entered,
):
    me = lax.axis_index("ctx")
    slab = lax.axis_index("slab")

    barrier = pltpu.get_barrier_semaphore()

    def greet_ctx(step, carry):
        pl.semaphore_signal(
            barrier, inc=1, device_id={"ctx": lax.rem(me + step, CTX)}, device_id_type=MESH
        )
        return carry

    zl, flat = lax.div(me, FLAT), lax.rem(me, FLAT)
    zh, yy = lax.div(slab, Y_ALL), lax.rem(slab, Y_ALL)
    depth = zh * Z_LO + zl
    at_plane = yy * FLAT + flat

    def in_plane(at):
        return {
            "ctx": zl * FLAT + lax.rem(at, FLAT),
            "slab": zh * Y_ALL + lax.div(at, FLAT),
        }

    def in_column(at):
        return {
            "ctx": lax.rem(at, Z_LO) * FLAT + flat,
            "slab": lax.div(at, Z_LO) * Y_ALL + yy,
        }

    def signal_each(semaphore, place, first_at, last_at):
        def body(at, carry):
            pl.semaphore_signal(semaphore, inc=1, device_id=place(at), device_id_type=MESH)
            return carry

        lax.fori_loop(first_at, last_at, body, 0)

    lax.fori_loop(FLAT, CTX, greet_ctx, 0)
    lax.fori_loop(1, FLAT, greet_ctx, 0)
    signal_each(barrier, in_plane, (yy + 1) * FLAT, PLANE)
    signal_each(barrier, in_column, (zh + 1) * Z_LO, Z_ALL)

    def load(source, target, at):
        copy = pltpu.make_async_copy(source, target, table_sem.at[at])
        copy.start()
        return copy

    gates = [
        load(source, target, at)
        for at, (source, target) in enumerate(
            [(key_hbm, key_ref), (value_hbm, value_ref), (grad_hbm, grad_ref), (query_hbm, query_ref)]
        )
    ]
    layers = [
        load(source, target, 4 + at)
        for at, (source, target) in enumerate(
            [
                (rot_hbm.at[me], rot),
                (w_first_hbm, w_first_ref),
                (b_first_hbm, b_first_ref),
                (freq_hbm, freq_ref),
                (w_second_hbm, w_second_ref),
                (decay_hbm, decay_ref),
                (skip_hbm, skip_ref),
                (stacked_hbm, stacked),
            ]
        )
    ]
    transforms = [
        load(source, target, 12 + at)
        for at, (source, target) in enumerate(
            [
                (first_hbm, first),
                (second_hbm, second),
                (second_inv_hbm, second_inv),
                (twiddle_hbm, twiddle),
                (first_t_hbm, first_t),
                (pair_hbm, pair),
            ]
        )
    ]

    def wait_loads(copies):
        for copy in copies:
            copy.wait()

    def send_all(source, target, at):
        def body(step, carry):
            peer = lax.rem(me + step, CTX)
            pltpu.make_async_remote_copy(
                src_ref=source.at[peer],
                dst_ref=target.at[me],
                send_sem=send_sem.at[at],
                recv_sem=recv_sem.at[at],
                device_id={"ctx": peer},
                device_id_type=MESH,
            ).start()
            return carry

        lax.fori_loop(1, CTX, body, 0)
        pltpu.make_async_copy(source.at[me], target.at[me], recv_sem.at[at]).start()

    def wait_all(target, at):
        pltpu.make_async_copy(target, target, recv_sem.at[at]).wait()

    def wait_sent(source, count, at):
        part = source.at[pl.ds(0, count)]
        pltpu.make_async_copy(part, part, send_sem.at[at]).wait()

    wait_loads(gates)
    skip_acc = jnp.zeros((CHAN, LANES), f32)
    for col in range(ROWS):
        lanes = pl.ds(col * LANES, LANES)
        mixed = key_ref[:, lanes].astype(f32) * value_ref[:, lanes].astype(f32)
        mixed = mixed.astype(bf16).astype(f32)
        mid = grad_ref[:, lanes].astype(f32) * query_ref[:, lanes].astype(f32)
        mid = mid.astype(bf16).astype(f32)
        flat_a[pl.ds(col, CHAN, stride=ROWS), :] = mixed
        flat_b[pl.ds(col, CHAN, stride=ROWS), :] = mid
        skip_acc = skip_acc + mixed * mid
    send_mg[:, 0] = flat_a[...].reshape(CHAN, ROWS, LANES).astype(bf16)
    send_mg[:, 1] = flat_b[...].reshape(CHAN, ROWS, LANES).astype(bf16)
    skip_sum = jnp.sum(skip_acc, axis=1, keepdims=True)

    wait_loads(layers)
    cos_at, sin_at = rot[0][:, :ORDER], rot[1][:, :ORDER]
    w_lin = w_first_ref[0:1, :]
    w_cos = w_first_ref[1 : 1 + BANDS, :]
    w_sin = w_first_ref[1 + BANDS : 1 + 2 * BANDS, :]
    start_frac = me.astype(f32) * (1.0 / CTX)
    weights[...] = jnp.zeros((KROWS, ORDER), f32)
    weights[0:BANDS, :] = w_cos * cos_at + w_sin * sin_at
    weights[BANDS : 2 * BANDS, :] = w_sin * cos_at - w_cos * sin_at
    weights[2 * BANDS : 2 * BANDS + 1, :] = w_lin
    freq_row = freq_ref[...].reshape(1, ORDER)
    weights[2 * BANDS + 1 : 2 * BANDS + 2, :] = (
        b_first_ref[...].reshape(1, ORDER) + w_lin * start_frac
    )
    scaled = weights[...] * (freq_row * (2.0 / math.pi))
    part_one = scaled.astype(bf16).astype(f32)
    rest = scaled - part_one
    part_two = rest.astype(bf16).astype(f32)
    part_three = (rest - part_two).astype(bf16).astype(f32)
    for at, part in enumerate([part_one, part_one, part_two, part_one, part_two, part_three]):
        weight_stack[at * KROWS : (at + 1) * KROWS, :] = part
    quarters[...] = dot_first(weight_stack[...].astype(bf16), stacked[...])
    decay_col = as_column(decay_ref[...].reshape(1, CHAN), CHAN)
    small = -2.0 * decay_col
    grown = small * (
        1.0 + small / 2 * (1.0 + small / 3 * (1.0 + small / 4 * (1.0 + small / 5 * (1.0 + small / 6))))
    )
    scaling = jnp.sqrt(grown / (jnp.exp(small * SEQ) - 1.0))
    wide = 256
    for col in range(PART // wide):
        lanes = pl.ds(col * wide, wide)
        sin_val, cos_val = sine_cosine(quarters[:, lanes])
        high, low = high_low(sin_val)
        hidden[0:ORDER, lanes] = high
        hidden[ORDER : 2 * ORDER, lanes] = low
        cosines[:, lanes] = cos_val
        times = lax.broadcasted_iota(jnp.int32, (CHAN, wide), 1) + (me * PART + col * wide)
        modul[:, lanes] = jnp.exp(-decay_col * times.astype(f32)) * scaling
    w_high, w_low = high_low(w_second_ref[...])
    filt = dot(jnp.concatenate([w_high, w_low], axis=0), hidden[0:ORDER, :])
    filt = filt[:CHAN] + filt[CHAN:] + dot(w_high, hidden[ORDER : 2 * ORDER, :])
    filt = filt * modul[...]
    for col in range(ROWS):
        flat_a[pl.ds(col, CHAN, stride=ROWS), :] = filt[:, col * LANES : (col + 1) * LANES]
    send_f[...] = flat_a[...].reshape(CHAN, ROWS, LANES).astype(bf16)

    pl.semaphore_wait(barrier, CTX - 1 + yy * FLAT + zh * Z_LO)
    send_all(send_mg, recv_mg, 0)
    signal_each(entered, in_plane, 0, yy * FLAT)
    signal_each(entered, in_column, 0, zh * Z_LO)

    wait_loads(transforms)
    wait_all(recv_mg, 0)
    both[:, 0:LANES] = recv_mg[:, 0].reshape(N_ONE, LANES)
    both[:, LANES : 2 * LANES] = recv_mg[:, 1].reshape(N_ONE, LANES)
    chunk = 256

    def turned(rows):
        return twiddle[rows, 0:LANES], twiddle[rows, LANES : 2 * LANES]

    def inverse_part(real, imag, cos_t, sin_t):
        back = dot(jnp.concatenate([real, imag], axis=1).astype(bf16), second_inv[...])
        c_real, c_imag = back[:, :LANES], back[:, LANES:]
        return (
            (c_real * cos_t - c_imag * sin_t).astype(bf16),
            (c_imag * cos_t + c_real * sin_t).astype(bf16),
        )

    def spectrum(a_real, a_imag, cos_t, sin_t):
        b_real = a_real * cos_t + a_imag * sin_t
        b_imag = a_imag * cos_t - a_real * sin_t
        return dot(jnp.concatenate([b_real, b_imag], axis=1).astype(bf16), second[...])

    for at in range(N_ONE // chunk):
        rows = pl.ds(at * chunk, chunk)
        low_rows = pl.ds(N_ONE + at * chunk, chunk)
        cos_t, sin_t = turned(rows)
        a_real = dot(first[rows, :], both[...])
        a_imag = dot(first[low_rows, :], both[...])
        w_spec = spectrum(a_real[:, :LANES], a_imag[:, :LANES], cos_t, sin_t)
        g_spec = spectrum(a_real[:, LANES:], a_imag[:, LANES:], cos_t, sin_t)
        spec_w[rows, :] = w_spec
        spec_g[rows, :] = g_spec
        w_r, w_i, g_r, g_i = w_spec[:, :LANES], w_spec[:, LANES:], g_spec[:, :LANES], g_spec[:, LANES:]
        d_real, d_imag = inverse_part(w_r * g_r + w_i * g_i, w_r * g_i - w_i * g_r, cos_t, sin_t)
        fold_a[rows, :] = d_real
        fold_a[low_rows, :] = d_imag
    group = CTX // 4
    for at in range(4):
        part = dot(first_t[at * N_ONE // 4 : (at + 1) * N_ONE // 4, :], fold_a[...])
        send_gf[at * group : (at + 1) * group] = part.astype(bf16).reshape(group, ROWS, LANES)

        def send_part(peer, carry):
            @pl.when(peer != me)
            def _():
                pltpu.make_async_remote_copy(
                    src_ref=send_gf.at[peer],
                    dst_ref=recv_gf.at[me],
                    send_sem=send_sem.at[2],
                    recv_sem=recv_sem.at[2],
                    device_id={"ctx": peer},
                    device_id_type=MESH,
                ).start()

            return carry

        lax.fori_loop(at * group, (at + 1) * group, send_part, 0)
    pltpu.make_async_copy(send_gf.at[me], recv_gf.at[me], recv_sem.at[2]).start()

    wait_all(recv_gf, 2)
    flat_a[...] = recv_gf[...].astype(f32).reshape(N_ONE, LANES)
    for col in range(ROWS):
        lanes = pl.ds(col * LANES, LANES)
        part = flat_a[pl.ds(col, CHAN, stride=ROWS), :] * modul[:, lanes]
        high, low = high_low(part)
        grad_mod[0:CHAN, lanes] = high
        grad_mod[CHAN : 2 * CHAN, lanes] = low
        grad_mod[2 * CHAN : 3 * CHAN, lanes] = high
    grad_hidden = dot_first(jnp.concatenate([w_high, w_high, w_low], axis=0), grad_mod[...])
    high, low = high_low(grad_hidden * cosines[...])
    grad_sin[0:ORDER, :] = high
    grad_sin[ORDER : 2 * ORDER, :] = low
    proj = dot_last(pair[...], grad_sin[0:ORDER, :])
    proj = proj[0:KROWS] + proj[48 : 48 + KROWS] + dot_last(pair[0:48, :], grad_sin[ORDER:, :])[0:KROWS]
    p_cos, p_sin = proj[0:BANDS], proj[BANDS : 2 * BANDS]
    p_lin, p_one = proj[2 * BANDS : 2 * BANDS + 1], proj[2 * BANDS + 1 : 2 * BANDS + 2]
    grad_first_rows = jnp.concatenate(
        [
            (p_cos * cos_at - p_sin * sin_at) * freq_row,
            (p_cos * sin_at + p_sin * cos_at) * freq_row,
        ],
        axis=0,
    )
    spare[...] = jnp.zeros((8, LANES), f32)
    spare[0:1, 0:ORDER] = (p_lin + start_frac * p_one) * freq_row
    spare[1:2, 0:ORDER] = p_one * freq_row
    spare[2:3, 0:ORDER] = jnp.sum(proj * weights[...], axis=0, keepdims=True)
    moved = pltpu.roll(spare[...], ORDER, 1)
    for at in range(PLANE):
        pay[at, :, 0:ORDER] = grad_first_rows[at : at + 1, :]
        pay[at, :, ORDER:LANES] = (
            moved[at : at + 1, ORDER:LANES] if at < 3 else jnp.zeros((1, ORDER), f32)
        )

    def send_each(source, target, slot, at, place, own, count, fixed):
        def body(step, carry):
            peer = lax.rem(own + step, count)
            pltpu.make_async_remote_copy(
                src_ref=source if fixed else source.at[peer],
                dst_ref=target.at[slot],
                send_sem=send_sem.at[at],
                recv_sem=recv_sem.at[at],
                device_id=place(peer),
                device_id_type=MESH,
            ).start()
            return carry

        lax.fori_loop(1, count, body, 0)
        pltpu.make_async_copy(
            source if fixed else source.at[own], target.at[slot], recv_sem.at[at]
        ).start()

    def in_ctx(at):
        return {"ctx": at}

    above = (Y_ALL - 1 - yy) * FLAT + (Z_HI - 1 - zh) * Z_LO

    @pl.when(above > 0)
    def _():
        pl.semaphore_wait(entered, above)

    send_each(pay, recv_p, at_plane, 4, in_plane, at_plane, PLANE, False)
    second_part = dot_last(grad_mod[0 : 2 * CHAN, :], hidden[...])
    high_part = second_part[:CHAN]
    low_part = jnp.where(
        lax.broadcasted_iota(jnp.int32, (CHAN, LANES), 1) < ORDER, second_part[CHAN:], 0.0
    )
    second_part = high_part + low_part
    second_part = second_part + pltpu.roll(second_part, ORDER, 1)
    for at in range(CTX):
        pay_own[at] = jnp.where(
            lax.broadcasted_iota(jnp.int32, (1, LANES), 1) < ORDER,
            second_part[at : at + 1, :],
            jnp.broadcast_to(skip_sum[at : at + 1, :], (1, LANES)),
        )
    send_each(pay_own, recv_own, me, 7, in_ctx, me, CTX, False)
    send_all(send_f, recv_f, 1)

    def add_up(ref, count):
        total = ref[0]
        for at in range(1, count):
            total = total + ref[at]
        return total

    wait_all(recv_p, 4)
    piece[...] = add_up(recv_p, PLANE)
    send_each(piece, recv_s, depth, 5, in_column, depth, Z_ALL, True)
    wait_all(recv_own, 7)
    done_own[...] = add_up(recv_own, CTX)
    send_each(done_own, all_own, me, 8, in_ctx, me, CTX, True)

    wait_all(recv_f, 1)
    for at in range(N_ONE // chunk):
        rows = pl.ds(at * chunk, chunk)
        low_rows = pl.ds(N_ONE + at * chunk, chunk)
        cos_t, sin_t = turned(rows)
        filt_c = recv_f[...].reshape(N_ONE, LANES)
        a_real = dot(first[rows, :], filt_c)
        a_imag = dot(first[low_rows, :], filt_c)
        h_spec = spectrum(a_real, a_imag, cos_t, sin_t)
        h_r, h_i = h_spec[:, :LANES], h_spec[:, LANES:]
        w_r, w_i = spec_w[rows, 0:LANES], spec_w[rows, LANES : 2 * LANES]
        g_r, g_i = spec_g[rows, 0:LANES], spec_g[rows, LANES : 2 * LANES]
        d_real, d_imag = inverse_part(h_r * w_r - h_i * w_i, h_r * w_i + h_i * w_r, cos_t, sin_t)
        fold_b[rows, 0:LANES] = d_real
        fold_b[low_rows, 0:LANES] = d_imag
        d_real, d_imag = inverse_part(h_r * g_r + h_i * g_i, h_r * g_i - h_i * g_r, cos_t, sin_t)
        fold_b[rows, LANES : 2 * LANES] = d_real
        fold_b[low_rows, LANES : 2 * LANES] = d_imag
    spread = lax.broadcasted_iota(jnp.int32, (1, CHAN), 1)
    my_skip = jnp.sum(
        jnp.where(spread == me, skip_ref[...].reshape(1, CHAN), 0.0), axis=1, keepdims=True
    )
    direct = dot(first_t[...], fold_b[...]) + my_skip * both[...].astype(f32)
    send_mb[:, 0] = direct[:, :LANES].astype(bf16).reshape(CTX, ROWS, LANES)
    send_mb[:, 1] = direct[:, LANES:].astype(bf16).reshape(CTX, ROWS, LANES)


    send_all(send_mb, recv_mb, 3)

    wait_all(recv_s, 5)
    done[...] = add_up(recv_s, Z_ALL)
    send_each(done, recv_d, at_plane, 6, in_plane, at_plane, PLANE, True)

    wait_all(recv_mb, 3)
    flat_a[...] = recv_mb[:, 0].astype(f32).reshape(N_ONE, LANES)
    flat_b[...] = recv_mb[:, 1].astype(f32).reshape(N_ONE, LANES)
    for col in range(ROWS):
        lanes = pl.ds(col * LANES, LANES)
        mid = flat_a[pl.ds(col, CHAN, stride=ROWS), :]
        back = flat_b[pl.ds(col, CHAN, stride=ROWS), :]
        query_out[:, lanes] = (grad_ref[:, lanes].astype(f32) * mid).astype(bf16)
        key_out[:, lanes] = (back * value_ref[:, lanes].astype(f32)).astype(bf16)
        value_out[:, lanes] = (back * key_ref[:, lanes].astype(f32)).astype(bf16)

    wait_sent(send_mg, CTX - 1, 0)
    wait_sent(send_f, CTX - 1, 1)
    wait_sent(send_gf, CTX - 1, 2)
    wait_sent(send_mb, CTX - 1, 3)
    wait_sent(pay, PLANE - 1, 4)
    wait_sent(recv_s, Z_ALL - 1, 5)
    wait_sent(pay_own, CTX - 1, 7)
    wait_sent(all_own, CTX - 1, 8)
    wait_all(all_own, 8)
    for at in range(CTX):
        sums_out[PLANE + at : PLANE + at + 1, :] = all_own[at]
    wait_all(recv_d, 6)
    for at in range(PLANE):
        sums_out[at : at + 1, :] = recv_d[at]
    wait_sent(recv_d, PLANE - 1, 6)


def last_kernel(
    query_ref,
    key_ref,
    value_ref,
    sums_ref,
    query_out,
    key_out,
    value_out,
    first_out,
    bias_out,
    freq_out,
    second_out,
    skip_out,
    first_ref,
    bias_ref,
    freq_ref,
    second_ref,
    skip_ref,
    sem,
):
    stores = []

    def store(source, target):
        copy = pltpu.make_async_copy(source, target, sem.at[len(stores)])
        copy.start()
        stores.append(copy)

    store(query_ref, query_out)
    store(key_ref, key_out)
    store(value_ref, value_out)
    first_ref[1 : 1 + 2 * BANDS, :] = sums_ref[0 : 2 * BANDS, 0:ORDER]
    upper = pltpu.roll(sums_ref[0:8, :], ORDER, 1)
    first_ref[0:1, :] = upper[0:1, 0:ORDER]
    store(first_ref, first_out)
    bias_ref[...] = upper[1:2, 0:ORDER].reshape(ORDER)
    store(bias_ref, bias_out)
    freq_ref[...] = upper[2:3, 0:ORDER].reshape(ORDER)
    store(freq_ref, freq_out)
    second_ref[...] = sums_ref[PLANE : PLANE + CHAN, 0:ORDER]
    store(second_ref, second_out)
    skip_row = as_row(sums_ref[PLANE : PLANE + CHAN, ORDER : ORDER + 1], CHAN)
    skip_ref[...] = skip_row.reshape(CHAN)
    store(skip_ref, skip_out)
    for copy in stores:
        copy.wait()


def shards(
    query_in,
    key_in,
    value_in,
    grad_out,
    w_first,
    b_first,
    frequency,
    w_second,
    decay_rate,
    skip_gain,
):
    consts = tables()
    vmem = pl.BlockSpec(memory_space=pltpu.VMEM)
    hbm = pl.BlockSpec(memory_space=pltpu.HBM)
    block = lambda *dims: pltpu.VMEM(dims, bf16)
    wide = lambda *dims: pltpu.VMEM(dims, f32)
    blocks = (CTX, ROWS, LANES)
    pairs = (CTX, 2, ROWS, LANES)
    rows = jax.ShapeDtypeStruct((CHAN, PART), bf16)
    sums_shape = jax.ShapeDtypeStruct((PLANE + CTX, LANES), f32)
    query_g, key_g, value_g, sums = pl.pallas_call(
        main_kernel,
        name="hyena_backward",
        out_shape=(rows, rows, rows, sums_shape),
        in_specs=[hbm] * 18,
        out_specs=(vmem, vmem, vmem, vmem),
        scratch_shapes=[
            block(CHAN, PART),
            block(CHAN, PART),
            block(CHAN, PART),
            block(CHAN, PART),
            wide(33, ORDER),
            wide(ORDER),
            wide(ORDER),
            wide(CHAN, ORDER),
            wide(CHAN),
            wide(CHAN),
            block(2 * N_ONE, N_ONE),
            block(N_ONE, 2 * N_ONE),
            block(2 * LANES, 2 * LANES),
            block(2 * LANES, 2 * LANES),
            wide(N_ONE, 2 * LANES),
            block(6 * KROWS, PART),
            block(96, PART),
            wide(2, BANDS, LANES),
            wide(N_ONE, LANES),
            wide(N_ONE, LANES),
            block(*pairs),
            block(*pairs),
            block(*blocks),
            block(*blocks),
            block(*blocks),
            block(*blocks),
            block(*pairs),
            block(*pairs),
            wide(KROWS, ORDER),
            wide(6 * KROWS, ORDER),
            wide(ORDER, PART),
            block(2 * ORDER, PART),
            wide(ORDER, PART),
            wide(CHAN, PART),
            block(N_ONE, 2 * LANES),
            wide(N_ONE, 2 * LANES),
            wide(N_ONE, 2 * LANES),
            block(2 * N_ONE, LANES),
            block(2 * N_ONE, 2 * LANES),
            block(3 * CHAN, PART),
            block(2 * ORDER, PART),
            wide(8, LANES),
            wide(PLANE, 1, LANES),
            wide(PLANE, 1, LANES),
            wide(1, LANES),
            wide(Z_ALL, 1, LANES),
            wide(1, LANES),
            wide(PLANE, 1, LANES),
            wide(CTX, 1, LANES),
            wide(CTX, 1, LANES),
            wide(1, LANES),
            wide(CTX, 1, LANES),
            pltpu.SemaphoreType.DMA((18,)),
            pltpu.SemaphoreType.DMA((9,)),
            pltpu.SemaphoreType.DMA((9,)),
            pltpu.SemaphoreType.REGULAR,
        ],
        compiler_params=pltpu.CompilerParams(
            collective_id=0, has_side_effects=True, vmem_limit_bytes=40 * 1024 * 1024
        ),
    )(
        *[pltpu.with_memory_space_constraint(held, pltpu.HBM) for held in (
        query_in,
        key_in,
        value_in,
        grad_out,
        w_first,
        b_first,
        frequency,
        w_second.T,
        decay_rate,
        skip_gain,
        *consts,
        )]
    )
    vector = lambda count: jax.ShapeDtypeStruct((count,), f32)
    outs = pl.pallas_call(
        last_kernel,
        name="results",
        out_shape=(
            rows,
            rows,
            rows,
            jax.ShapeDtypeStruct((33, ORDER), f32),
            vector(ORDER),
            vector(ORDER),
            jax.ShapeDtypeStruct((CHAN, ORDER), f32),
            vector(CHAN),
        ),
        in_specs=[vmem] * 4,
        out_specs=tuple([hbm] * 8),
        scratch_shapes=[
            wide(33, ORDER),
            wide(ORDER),
            wide(ORDER),
            wide(CHAN, ORDER),
            wide(CHAN),
            pltpu.SemaphoreType.DMA((8,)),
        ],
        compiler_params=pltpu.CompilerParams(vmem_limit_bytes=56 * 1024 * 1024),
    )(*[pltpu.with_memory_space_constraint(held, pltpu.VMEM) for held in (query_g, key_g, value_g, sums)])
    return (*outs[:6], outs[6].T, outs[7])


def solution(mesh):
    placed = (
        P("slab", "ctx"),
        P("slab", "ctx"),
        P("slab", "ctx"),
        P("slab", "ctx"),
        P(),
        P(),
        P(),
        P(None, "slab"),
        P("slab"),
        P("slab"),
    )
    return jax.shard_map(
        shards,
        mesh=mesh,
        in_specs=placed,
        out_specs=(
            P("slab", "ctx"),
            P("slab", "ctx"),
            P("slab", "ctx"),
            P(),
            P(),
            P(),
            P(None, "slab"),
            P("slab"),
        ),
        check_vma=False,
    )
```

```python
import math

import jax
import jax.numpy as jnp
import ml_dtypes
import numpy as np
from jax import lax
from jax.experimental import pallas as pl
from jax.experimental.pallas import tpu as pltpu
from jax.sharding import PartitionSpec as P

BANDS = 16
CTX = 32
SLAB = 16
CHAN = 32
PART = 2048
SEQ = CTX * PART
ROWS = 16
LANES = 128
N_ONE = SEQ // LANES
ORDER = 64
KROWS = 40
Z_LO, Z_HI, Y_ALL, FLAT = 4, 4, 4, 8
PLANE = Y_ALL * FLAT
Z_ALL = Z_HI * Z_LO

MESH = pl.DeviceIdType.MESH
f32, bf16 = jnp.float32, jnp.bfloat16


def np_parts(table, count):
    out, rest = [], np.asarray(table, np.float64)
    for _ in range(count):
        part = rest.astype(np.float32).astype(ml_dtypes.bfloat16)
        out.append(part)
        rest = rest - part.astype(np.float64)
    return out


def tables():
    k_one = np.arange(N_ONE)[:, None]
    n_one = np.arange(N_ONE)[None, :]
    phase = 2 * np.pi * (((4 * k_one + 1) * n_one) % (4 * N_ONE)) / (4 * N_ONE)
    first = np.concatenate([np.cos(phase), -np.sin(phase)], axis=0)
    n_two = np.arange(LANES)[None, :]
    turn = 2 * np.pi * (k_one + 0.25) * n_two / SEQ
    twiddle = np.concatenate([np.cos(turn), np.sin(turn)], axis=1).astype(np.float32)
    small = 2 * np.pi * ((np.arange(LANES)[:, None] * n_two) % LANES) / LANES
    cos_s, sin_s = np.cos(small), np.sin(small)
    second = np.block([[cos_s, -sin_s], [sin_s, cos_s]])
    second_inv = np.block([[cos_s, sin_s], [-sin_s, cos_s]])
    place = np.arange(PART)
    bands = np.arange(1, BANDS + 1)
    arc = 2 * np.pi * (bands[:, None] * place[None, :] % SEQ) / SEQ
    base = np.zeros((KROWS, PART))
    base[:BANDS], base[BANDS : 2 * BANDS] = np.cos(arc), np.sin(arc)
    base[2 * BANDS], base[2 * BANDS + 1] = place / SEQ, 1.0
    b_one, b_two, b_three = np_parts(base, 3)
    stacked = np.concatenate([b_one, b_two, b_one, b_three, b_two, b_one], axis=0)
    pair = np.zeros((96, PART), ml_dtypes.bfloat16)
    pair[:KROWS], pair[48 : 48 + KROWS] = b_one, b_two
    start = 2 * np.pi * (bands[None, :] * np.arange(CTX)[:, None] % CTX) / CTX
    rot = np.stack([np.cos(start), np.sin(start)], axis=1).astype(np.float32)
    rot = np.broadcast_to(rot[:, :, :, None], (CTX, 2, BANDS, LANES)).copy()
    one = lambda table: np_parts(table, 1)[0]
    return (
        one(first),
        one(first.T / SEQ),
        one(second),
        one(second_inv),
        twiddle,
        stacked,
        pair,
        rot,
    )


def dot(left, right):
    return jnp.dot(left, right, preferred_element_type=f32)


def dot_first(left, right):
    return lax.dot_general(left, right, (((0,), (0,)), ((), ())), preferred_element_type=f32)


def dot_last(left, right):
    return lax.dot_general(left, right, (((1,), (1,)), ((), ())), preferred_element_type=f32)


def high_low(value):
    high = value.astype(bf16)
    return high, (value - high.astype(f32)).astype(bf16)


def eye(count):
    rows = lax.broadcasted_iota(jnp.int32, (count, count), 0)
    return rows == lax.broadcasted_iota(jnp.int32, (count, count), 1)


def as_column(row, count):
    spread = jnp.broadcast_to(row, (count, count))
    return jnp.sum(jnp.where(eye(count), spread, 0.0), axis=1, keepdims=True)


def as_row(column, count):
    spread = jnp.broadcast_to(column, (count, count))
    return jnp.sum(jnp.where(eye(count), spread, 0.0), axis=0, keepdims=True)


def sine_cosine(quarters):
    whole = jnp.floor(quarters + 0.5)
    rest = quarters - whole
    turn = whole.astype(jnp.int32)
    angle = rest * (math.pi / 2)
    square = angle * angle
    sine = angle + angle * square * (
        -1.0 / 6 + square * (1.0 / 120 + square * (-1.0 / 5040 + square * (1.0 / 362880)))
    )
    cosine = 1.0 + square * (
        -0.5 + square * (1.0 / 24 + square * (-1.0 / 720 + square * (1.0 / 40320)))
    )
    swap = (turn & 1) == 1
    sin_val = jnp.where(swap, cosine, sine)
    cos_val = jnp.where(swap, sine, cosine)
    sin_val = jnp.where((turn & 2) == 2, -sin_val, sin_val)
    cos_val = jnp.where(((turn + 1) & 2) == 2, -cos_val, cos_val)
    return sin_val, cos_val


def main_kernel(
    query_hbm,
    key_hbm,
    value_hbm,
    grad_hbm,
    w_first_hbm,
    b_first_hbm,
    freq_hbm,
    w_second_hbm,
    decay_hbm,
    skip_hbm,
    first_hbm,
    first_t_hbm,
    second_hbm,
    second_inv_hbm,
    twiddle_hbm,
    stacked_hbm,
    pair_hbm,
    rot_hbm,
    query_out,
    key_out,
    value_out,
    sums_out,
    query_ref,
    key_ref,
    value_ref,
    grad_ref,
    w_first_ref,
    b_first_ref,
    freq_ref,
    w_second_ref,
    decay_ref,
    skip_ref,
    first,
    first_t,
    second,
    second_inv,
    twiddle,
    stacked,
    pair,
    rot,
    flat_a,
    flat_b,
    send_mg,
    recv_mg,
    send_f,
    recv_f,
    send_gf,
    recv_gf,
    send_mb,
    recv_mb,
    weights,
    weight_stack,
    quarters,
    hidden,
    cosines,
    modul,
    both,
    partial,
    spec_w,
    spec_g,
    fold_a,
    fold_b,
    grad_mod,
    grad_sin,
    spare,
    pay,
    recv_p,
    piece,
    recv_s,
    done,
    recv_d,
    pay_own,
    recv_own,
    done_own,
    all_own,
    table_sem,
    send_sem,
    recv_sem,
    entered,
):
    me = lax.axis_index("ctx")
    slab = lax.axis_index("slab")

    barrier = pltpu.get_barrier_semaphore()

    def greet_ctx(step, carry):
        pl.semaphore_signal(
            barrier, inc=1, device_id={"ctx": lax.rem(me + step, CTX)}, device_id_type=MESH
        )
        return carry

    zl, flat = lax.div(me, FLAT), lax.rem(me, FLAT)
    zh, yy = lax.div(slab, Y_ALL), lax.rem(slab, Y_ALL)
    depth = zh * Z_LO + zl
    at_plane = yy * FLAT + flat

    def in_plane(at):
        return {
            "ctx": zl * FLAT + lax.rem(at, FLAT),
            "slab": zh * Y_ALL + lax.div(at, FLAT),
        }

    def in_column(at):
        return {
            "ctx": lax.rem(at, Z_LO) * FLAT + flat,
            "slab": lax.div(at, Z_LO) * Y_ALL + yy,
        }

    def signal_each(semaphore, place, first_at, last_at):
        def body(at, carry):
            pl.semaphore_signal(semaphore, inc=1, device_id=place(at), device_id_type=MESH)
            return carry

        lax.fori_loop(first_at, last_at, body, 0)

    lax.fori_loop(FLAT, CTX, greet_ctx, 0)
    lax.fori_loop(1, FLAT, greet_ctx, 0)
    signal_each(barrier, in_plane, (yy + 1) * FLAT, PLANE)
    signal_each(barrier, in_column, (zh + 1) * Z_LO, Z_ALL)

    def load(source, target, at):
        copy = pltpu.make_async_copy(source, target, table_sem.at[at])
        copy.start()
        return copy

    gates = [
        load(source, target, at)
        for at, (source, target) in enumerate(
            [(key_hbm, key_ref), (value_hbm, value_ref), (grad_hbm, grad_ref), (query_hbm, query_ref)]
        )
    ]
    layers = [
        load(source, target, 4 + at)
        for at, (source, target) in enumerate(
            [
                (rot_hbm.at[me], rot),
                (w_first_hbm, w_first_ref),
                (b_first_hbm, b_first_ref),
                (freq_hbm, freq_ref),
                (w_second_hbm, w_second_ref),
                (decay_hbm, decay_ref),
                (skip_hbm, skip_ref),
                (stacked_hbm, stacked),
            ]
        )
    ]
    transforms = [
        load(source, target, 12 + at)
        for at, (source, target) in enumerate(
            [
                (first_hbm, first),
                (second_hbm, second),
                (second_inv_hbm, second_inv),
                (twiddle_hbm, twiddle),
                (first_t_hbm, first_t),
                (pair_hbm, pair),
            ]
        )
    ]

    def wait_loads(copies):
        for copy in copies:
            copy.wait()

    def send_all(source, target, at, arrival=None):
        arrival = at if arrival is None else arrival

        def body(step, carry):
            peer = lax.rem(me + step, CTX)
            pltpu.make_async_remote_copy(
                src_ref=source.at[peer],
                dst_ref=target.at[me],
                send_sem=send_sem.at[at],
                recv_sem=recv_sem.at[arrival],
                device_id={"ctx": peer},
                device_id_type=MESH,
            ).start()
            return carry

        lax.fori_loop(1, CTX, body, 0)
        pltpu.make_async_copy(source.at[me], target.at[me], recv_sem.at[arrival]).start()

    def wait_all(target, at):
        pltpu.make_async_copy(target, target, recv_sem.at[at]).wait()

    def wait_sent(source, count, at):
        part = source.at[pl.ds(0, count)]
        pltpu.make_async_copy(part, part, send_sem.at[at]).wait()

    wait_loads(gates)
    skip_acc = jnp.zeros((CHAN, LANES), f32)
    for col in range(ROWS):
        lanes = pl.ds(col * LANES, LANES)
        mixed = key_ref[:, lanes].astype(f32) * value_ref[:, lanes].astype(f32)
        mixed = mixed.astype(bf16).astype(f32)
        mid = grad_ref[:, lanes].astype(f32) * query_ref[:, lanes].astype(f32)
        mid = mid.astype(bf16).astype(f32)
        flat_a[pl.ds(col, CHAN, stride=ROWS), :] = mixed
        flat_b[pl.ds(col, CHAN, stride=ROWS), :] = mid
        skip_acc = skip_acc + mixed * mid
    send_mg[:, 0] = flat_a[...].reshape(CHAN, ROWS, LANES).astype(bf16)
    send_mg[:, 1] = flat_b[...].reshape(CHAN, ROWS, LANES).astype(bf16)
    skip_sum = jnp.sum(skip_acc, axis=1, keepdims=True)

    wait_loads(layers)
    cos_at, sin_at = rot[0][:, :ORDER], rot[1][:, :ORDER]
    w_lin = w_first_ref[0:1, :]
    w_cos = w_first_ref[1 : 1 + BANDS, :]
    w_sin = w_first_ref[1 + BANDS : 1 + 2 * BANDS, :]
    start_frac = me.astype(f32) * (1.0 / CTX)
    weights[...] = jnp.zeros((KROWS, ORDER), f32)
    weights[0:BANDS, :] = w_cos * cos_at + w_sin * sin_at
    weights[BANDS : 2 * BANDS, :] = w_sin * cos_at - w_cos * sin_at
    weights[2 * BANDS : 2 * BANDS + 1, :] = w_lin
    freq_row = freq_ref[...].reshape(1, ORDER)
    weights[2 * BANDS + 1 : 2 * BANDS + 2, :] = (
        b_first_ref[...].reshape(1, ORDER) + w_lin * start_frac
    )
    scaled = weights[...] * (freq_row * (2.0 / math.pi))
    part_one = scaled.astype(bf16).astype(f32)
    rest = scaled - part_one
    part_two = rest.astype(bf16).astype(f32)
    part_three = (rest - part_two).astype(bf16).astype(f32)
    for at, part in enumerate([part_one, part_one, part_two, part_one, part_two, part_three]):
        weight_stack[at * KROWS : (at + 1) * KROWS, :] = part
    quarters[...] = dot_first(weight_stack[...].astype(bf16), stacked[...])
    decay_col = as_column(decay_ref[...].reshape(1, CHAN), CHAN)
    small = -2.0 * decay_col
    grown = small * (
        1.0 + small / 2 * (1.0 + small / 3 * (1.0 + small / 4 * (1.0 + small / 5 * (1.0 + small / 6))))
    )
    scaling = jnp.sqrt(grown / (jnp.exp(small * SEQ) - 1.0))
    wide = 256
    for col in range(PART // wide):
        lanes = pl.ds(col * wide, wide)
        sin_val, cos_val = sine_cosine(quarters[:, lanes])
        high, low = high_low(sin_val)
        hidden[0:ORDER, lanes] = high
        hidden[ORDER : 2 * ORDER, lanes] = low
        cosines[:, lanes] = cos_val
        times = lax.broadcasted_iota(jnp.int32, (CHAN, wide), 1) + (me * PART + col * wide)
        modul[:, lanes] = jnp.exp(-decay_col * times.astype(f32)) * scaling
    w_high, w_low = high_low(w_second_ref[...])
    filt = dot(jnp.concatenate([w_high, w_low], axis=0), hidden[0:ORDER, :])
    filt = filt[:CHAN] + filt[CHAN:] + dot(w_high, hidden[ORDER : 2 * ORDER, :])
    filt = filt * modul[...]
    for col in range(ROWS):
        flat_a[pl.ds(col, CHAN, stride=ROWS), :] = filt[:, col * LANES : (col + 1) * LANES]
    send_f[...] = flat_a[...].reshape(CHAN, ROWS, LANES).astype(bf16)

    pl.semaphore_wait(barrier, CTX - 1 + yy * FLAT + zh * Z_LO)
    send_all(send_mg, recv_mg, 0, 9 + zl)
    signal_each(entered, in_plane, 0, yy * FLAT)
    signal_each(entered, in_column, 0, zh * Z_LO)

    wait_loads(transforms)
    for at in range(Z_LO):
        group = lax.rem(zl + Z_LO - at, Z_LO)
        sources = pl.ds(group * FLAT, FLAT)
        arrived = recv_mg.at[sources]
        pltpu.make_async_copy(arrived, arrived, recv_sem.at[9 + group]).wait()
        inner = pl.ds(pl.multiple_of(group * LANES, LANES), LANES)
        both[inner, 0:LANES] = recv_mg[sources, 0].reshape(LANES, LANES)
        both[inner, LANES : 2 * LANES] = recv_mg[sources, 1].reshape(LANES, LANES)
        if at == 0:
            partial[...] = dot(first[:, inner], both[inner, :])
        elif at < Z_LO - 1:
            partial[...] += dot(first[:, inner], both[inner, :])
    chunk = 256

    def turned(rows):
        return twiddle[rows, 0:LANES], twiddle[rows, LANES : 2 * LANES]

    def inverse_part(real, imag, cos_t, sin_t):
        back = dot(jnp.concatenate([real, imag], axis=1).astype(bf16), second_inv[...])
        c_real, c_imag = back[:, :LANES], back[:, LANES:]
        return (
            (c_real * cos_t - c_imag * sin_t).astype(bf16),
            (c_imag * cos_t + c_real * sin_t).astype(bf16),
        )

    def spectrum(a_real, a_imag, cos_t, sin_t):
        b_real = a_real * cos_t + a_imag * sin_t
        b_imag = a_imag * cos_t - a_real * sin_t
        return dot(jnp.concatenate([b_real, b_imag], axis=1).astype(bf16), second[...])

    for at in range(N_ONE // chunk):
        rows = pl.ds(at * chunk, chunk)
        low_rows = pl.ds(N_ONE + at * chunk, chunk)
        cos_t, sin_t = turned(rows)
        a_real = partial[rows, :] + dot(first[rows, inner], both[inner, :])
        a_imag = partial[low_rows, :] + dot(first[low_rows, inner], both[inner, :])
        w_spec = spectrum(a_real[:, :LANES], a_imag[:, :LANES], cos_t, sin_t)
        g_spec = spectrum(a_real[:, LANES:], a_imag[:, LANES:], cos_t, sin_t)
        spec_w[rows, :] = w_spec
        spec_g[rows, :] = g_spec
        w_r, w_i, g_r, g_i = w_spec[:, :LANES], w_spec[:, LANES:], g_spec[:, :LANES], g_spec[:, LANES:]
        d_real, d_imag = inverse_part(w_r * g_r + w_i * g_i, w_r * g_i - w_i * g_r, cos_t, sin_t)
        fold_a[rows, :] = d_real
        fold_a[low_rows, :] = d_imag
    group = CTX // 4
    for at in range(4):
        part = dot(first_t[at * N_ONE // 4 : (at + 1) * N_ONE // 4, :], fold_a[...])
        send_gf[at * group : (at + 1) * group] = part.astype(bf16).reshape(group, ROWS, LANES)

        def send_part(peer, carry):
            @pl.when(peer != me)
            def _():
                pltpu.make_async_remote_copy(
                    src_ref=send_gf.at[peer],
                    dst_ref=recv_gf.at[me],
                    send_sem=send_sem.at[2],
                    recv_sem=recv_sem.at[2],
                    device_id={"ctx": peer},
                    device_id_type=MESH,
                ).start()

            return carry

        lax.fori_loop(at * group, (at + 1) * group, send_part, 0)
    pltpu.make_async_copy(send_gf.at[me], recv_gf.at[me], recv_sem.at[2]).start()

    wait_all(recv_gf, 2)
    flat_a[...] = recv_gf[...].astype(f32).reshape(N_ONE, LANES)
    for col in range(ROWS):
        lanes = pl.ds(col * LANES, LANES)
        part = flat_a[pl.ds(col, CHAN, stride=ROWS), :] * modul[:, lanes]
        high, low = high_low(part)
        grad_mod[0:CHAN, lanes] = high
        grad_mod[CHAN : 2 * CHAN, lanes] = low
        grad_mod[2 * CHAN : 3 * CHAN, lanes] = high
    grad_hidden = dot_first(jnp.concatenate([w_high, w_high, w_low], axis=0), grad_mod[...])
    high, low = high_low(grad_hidden * cosines[...])
    grad_sin[0:ORDER, :] = high
    grad_sin[ORDER : 2 * ORDER, :] = low
    proj = dot_last(pair[...], grad_sin[0:ORDER, :])
    proj = proj[0:KROWS] + proj[48 : 48 + KROWS] + dot_last(pair[0:48, :], grad_sin[ORDER:, :])[0:KROWS]
    p_cos, p_sin = proj[0:BANDS], proj[BANDS : 2 * BANDS]
    p_lin, p_one = proj[2 * BANDS : 2 * BANDS + 1], proj[2 * BANDS + 1 : 2 * BANDS + 2]
    grad_first_rows = jnp.concatenate(
        [
            (p_cos * cos_at - p_sin * sin_at) * freq_row,
            (p_cos * sin_at + p_sin * cos_at) * freq_row,
        ],
        axis=0,
    )
    spare[...] = jnp.zeros((8, LANES), f32)
    spare[0:1, 0:ORDER] = (p_lin + start_frac * p_one) * freq_row
    spare[1:2, 0:ORDER] = p_one * freq_row
    spare[2:3, 0:ORDER] = jnp.sum(proj * weights[...], axis=0, keepdims=True)
    moved = pltpu.roll(spare[...], ORDER, 1)
    for at in range(PLANE):
        pay[at, :, 0:ORDER] = grad_first_rows[at : at + 1, :]
        pay[at, :, ORDER:LANES] = (
            moved[at : at + 1, ORDER:LANES] if at < 3 else jnp.zeros((1, ORDER), f32)
        )

    def send_each(source, target, slot, at, place, own, count, fixed):
        def body(step, carry):
            peer = lax.rem(own + step, count)
            pltpu.make_async_remote_copy(
                src_ref=source if fixed else source.at[peer],
                dst_ref=target.at[slot],
                send_sem=send_sem.at[at],
                recv_sem=recv_sem.at[at],
                device_id=place(peer),
                device_id_type=MESH,
            ).start()
            return carry

        lax.fori_loop(1, count, body, 0)
        pltpu.make_async_copy(
            source if fixed else source.at[own], target.at[slot], recv_sem.at[at]
        ).start()

    def in_ctx(at):
        return {"ctx": at}

    above = (Y_ALL - 1 - yy) * FLAT + (Z_HI - 1 - zh) * Z_LO

    @pl.when(above > 0)
    def _():
        pl.semaphore_wait(entered, above)

    send_each(pay, recv_p, at_plane, 4, in_plane, at_plane, PLANE, False)
    second_part = dot_last(grad_mod[0 : 2 * CHAN, :], hidden[...])
    high_part = second_part[:CHAN]
    low_part = jnp.where(
        lax.broadcasted_iota(jnp.int32, (CHAN, LANES), 1) < ORDER, second_part[CHAN:], 0.0
    )
    second_part = high_part + low_part
    second_part = second_part + pltpu.roll(second_part, ORDER, 1)
    for at in range(CTX):
        pay_own[at] = jnp.where(
            lax.broadcasted_iota(jnp.int32, (1, LANES), 1) < ORDER,
            second_part[at : at + 1, :],
            jnp.broadcast_to(skip_sum[at : at + 1, :], (1, LANES)),
        )
    send_each(pay_own, recv_own, me, 7, in_ctx, me, CTX, False)
    send_all(send_f, recv_f, 1)

    def add_up(ref, count):
        total = ref[0]
        for at in range(1, count):
            total = total + ref[at]
        return total

    wait_all(recv_p, 4)
    piece[...] = add_up(recv_p, PLANE)
    send_each(piece, recv_s, depth, 5, in_column, depth, Z_ALL, True)
    wait_all(recv_own, 7)
    done_own[...] = add_up(recv_own, CTX)
    send_each(done_own, all_own, me, 8, in_ctx, me, CTX, True)

    wait_all(recv_f, 1)
    for at in range(N_ONE // chunk):
        rows = pl.ds(at * chunk, chunk)
        low_rows = pl.ds(N_ONE + at * chunk, chunk)
        cos_t, sin_t = turned(rows)
        filt_c = recv_f[...].reshape(N_ONE, LANES)
        a_real = dot(first[rows, :], filt_c)
        a_imag = dot(first[low_rows, :], filt_c)
        h_spec = spectrum(a_real, a_imag, cos_t, sin_t)
        h_r, h_i = h_spec[:, :LANES], h_spec[:, LANES:]
        w_r, w_i = spec_w[rows, 0:LANES], spec_w[rows, LANES : 2 * LANES]
        g_r, g_i = spec_g[rows, 0:LANES], spec_g[rows, LANES : 2 * LANES]
        d_real, d_imag = inverse_part(h_r * w_r - h_i * w_i, h_r * w_i + h_i * w_r, cos_t, sin_t)
        fold_b[rows, 0:LANES] = d_real
        fold_b[low_rows, 0:LANES] = d_imag
        d_real, d_imag = inverse_part(h_r * g_r + h_i * g_i, h_r * g_i - h_i * g_r, cos_t, sin_t)
        fold_b[rows, LANES : 2 * LANES] = d_real
        fold_b[low_rows, LANES : 2 * LANES] = d_imag
    spread = lax.broadcasted_iota(jnp.int32, (1, CHAN), 1)
    my_skip = jnp.sum(
        jnp.where(spread == me, skip_ref[...].reshape(1, CHAN), 0.0), axis=1, keepdims=True
    )
    direct = dot(first_t[...], fold_b[...]) + my_skip * both[...].astype(f32)
    send_mb[:, 0] = direct[:, :LANES].astype(bf16).reshape(CTX, ROWS, LANES)
    send_mb[:, 1] = direct[:, LANES:].astype(bf16).reshape(CTX, ROWS, LANES)


    send_all(send_mb, recv_mb, 3)

    wait_all(recv_s, 5)
    done[...] = add_up(recv_s, Z_ALL)
    send_each(done, recv_d, at_plane, 6, in_plane, at_plane, PLANE, True)

    wait_all(recv_mb, 3)
    flat_a[...] = recv_mb[:, 0].astype(f32).reshape(N_ONE, LANES)
    flat_b[...] = recv_mb[:, 1].astype(f32).reshape(N_ONE, LANES)
    for col in range(ROWS):
        lanes = pl.ds(col * LANES, LANES)
        mid = flat_a[pl.ds(col, CHAN, stride=ROWS), :]
        back = flat_b[pl.ds(col, CHAN, stride=ROWS), :]
        query_out[:, lanes] = (grad_ref[:, lanes].astype(f32) * mid).astype(bf16)
        key_out[:, lanes] = (back * value_ref[:, lanes].astype(f32)).astype(bf16)
        value_out[:, lanes] = (back * key_ref[:, lanes].astype(f32)).astype(bf16)

    wait_sent(send_mg, CTX - 1, 0)
    wait_sent(send_f, CTX - 1, 1)
    wait_sent(send_gf, CTX - 1, 2)
    wait_sent(send_mb, CTX - 1, 3)
    wait_sent(pay, PLANE - 1, 4)
    wait_sent(recv_s, Z_ALL - 1, 5)
    wait_sent(pay_own, CTX - 1, 7)
    wait_sent(all_own, CTX - 1, 8)
    wait_all(all_own, 8)
    for at in range(CTX):
        sums_out[PLANE + at : PLANE + at + 1, :] = all_own[at]
    wait_all(recv_d, 6)
    for at in range(PLANE):
        sums_out[at : at + 1, :] = recv_d[at]
    wait_sent(recv_d, PLANE - 1, 6)


def last_kernel(
    query_ref,
    key_ref,
    value_ref,
    sums_ref,
    query_out,
    key_out,
    value_out,
    first_out,
    bias_out,
    freq_out,
    second_out,
    skip_out,
    first_ref,
    bias_ref,
    freq_ref,
    second_ref,
    skip_ref,
    sem,
):
    stores = []

    def store(source, target):
        copy = pltpu.make_async_copy(source, target, sem.at[len(stores)])
        copy.start()
        stores.append(copy)

    store(query_ref, query_out)
    store(key_ref, key_out)
    store(value_ref, value_out)
    first_ref[1 : 1 + 2 * BANDS, :] = sums_ref[0 : 2 * BANDS, 0:ORDER]
    upper = pltpu.roll(sums_ref[0:8, :], ORDER, 1)
    first_ref[0:1, :] = upper[0:1, 0:ORDER]
    store(first_ref, first_out)
    bias_ref[...] = upper[1:2, 0:ORDER].reshape(ORDER)
    store(bias_ref, bias_out)
    freq_ref[...] = upper[2:3, 0:ORDER].reshape(ORDER)
    store(freq_ref, freq_out)
    second_ref[...] = sums_ref[PLANE : PLANE + CHAN, 0:ORDER]
    store(second_ref, second_out)
    skip_row = as_row(sums_ref[PLANE : PLANE + CHAN, ORDER : ORDER + 1], CHAN)
    skip_ref[...] = skip_row.reshape(CHAN)
    store(skip_ref, skip_out)
    for copy in stores:
        copy.wait()


def shards(
    query_in,
    key_in,
    value_in,
    grad_out,
    w_first,
    b_first,
    frequency,
    w_second,
    decay_rate,
    skip_gain,
):
    consts = tables()
    vmem = pl.BlockSpec(memory_space=pltpu.VMEM)
    hbm = pl.BlockSpec(memory_space=pltpu.HBM)
    block = lambda *dims: pltpu.VMEM(dims, bf16)
    wide = lambda *dims: pltpu.VMEM(dims, f32)
    blocks = (CTX, ROWS, LANES)
    pairs = (CTX, 2, ROWS, LANES)
    rows = jax.ShapeDtypeStruct((CHAN, PART), bf16)
    sums_shape = jax.ShapeDtypeStruct((PLANE + CTX, LANES), f32)
    query_g, key_g, value_g, sums = pl.pallas_call(
        main_kernel,
        name="hyena_backward",
        out_shape=(rows, rows, rows, sums_shape),
        in_specs=[hbm] * 18,
        out_specs=(vmem, vmem, vmem, vmem),
        scratch_shapes=[
            block(CHAN, PART),
            block(CHAN, PART),
            block(CHAN, PART),
            block(CHAN, PART),
            wide(33, ORDER),
            wide(ORDER),
            wide(ORDER),
            wide(CHAN, ORDER),
            wide(CHAN),
            wide(CHAN),
            block(2 * N_ONE, N_ONE),
            block(N_ONE, 2 * N_ONE),
            block(2 * LANES, 2 * LANES),
            block(2 * LANES, 2 * LANES),
            wide(N_ONE, 2 * LANES),
            block(6 * KROWS, PART),
            block(96, PART),
            wide(2, BANDS, LANES),
            wide(N_ONE, LANES),
            wide(N_ONE, LANES),
            block(*pairs),
            block(*pairs),
            block(*blocks),
            block(*blocks),
            block(*blocks),
            block(*blocks),
            block(*pairs),
            block(*pairs),
            wide(KROWS, ORDER),
            wide(6 * KROWS, ORDER),
            wide(ORDER, PART),
            block(2 * ORDER, PART),
            wide(ORDER, PART),
            wide(CHAN, PART),
            block(N_ONE, 2 * LANES),
            wide(2 * N_ONE, 2 * LANES),
            wide(N_ONE, 2 * LANES),
            wide(N_ONE, 2 * LANES),
            block(2 * N_ONE, LANES),
            block(2 * N_ONE, 2 * LANES),
            block(3 * CHAN, PART),
            block(2 * ORDER, PART),
            wide(8, LANES),
            wide(PLANE, 1, LANES),
            wide(PLANE, 1, LANES),
            wide(1, LANES),
            wide(Z_ALL, 1, LANES),
            wide(1, LANES),
            wide(PLANE, 1, LANES),
            wide(CTX, 1, LANES),
            wide(CTX, 1, LANES),
            wide(1, LANES),
            wide(CTX, 1, LANES),
            pltpu.SemaphoreType.DMA((18,)),
            pltpu.SemaphoreType.DMA((9,)),
            pltpu.SemaphoreType.DMA((13,)),
            pltpu.SemaphoreType.REGULAR,
        ],
        compiler_params=pltpu.CompilerParams(
            collective_id=0, has_side_effects=True, vmem_limit_bytes=40 * 1024 * 1024
        ),
    )(
        *[pltpu.with_memory_space_constraint(held, pltpu.HBM) for held in (
        query_in,
        key_in,
        value_in,
        grad_out,
        w_first,
        b_first,
        frequency,
        w_second.T,
        decay_rate,
        skip_gain,
        *consts,
        )]
    )
    vector = lambda count: jax.ShapeDtypeStruct((count,), f32)
    outs = pl.pallas_call(
        last_kernel,
        name="results",
        out_shape=(
            rows,
            rows,
            rows,
            jax.ShapeDtypeStruct((33, ORDER), f32),
            vector(ORDER),
            vector(ORDER),
            jax.ShapeDtypeStruct((CHAN, ORDER), f32),
            vector(CHAN),
        ),
        in_specs=[vmem] * 4,
        out_specs=tuple([hbm] * 8),
        scratch_shapes=[
            wide(33, ORDER),
            wide(ORDER),
            wide(ORDER),
            wide(CHAN, ORDER),
            wide(CHAN),
            pltpu.SemaphoreType.DMA((8,)),
        ],
        compiler_params=pltpu.CompilerParams(vmem_limit_bytes=56 * 1024 * 1024),
    )(*[pltpu.with_memory_space_constraint(held, pltpu.VMEM) for held in (query_g, key_g, value_g, sums)])
    return (*outs[:6], outs[6].T, outs[7])


def solution(mesh):
    placed = (
        P("slab", "ctx"),
        P("slab", "ctx"),
        P("slab", "ctx"),
        P("slab", "ctx"),
        P(),
        P(),
        P(),
        P(None, "slab"),
        P("slab"),
        P("slab"),
    )
    return jax.shard_map(
        shards,
        mesh=mesh,
        in_specs=placed,
        out_specs=(
            P("slab", "ctx"),
            P("slab", "ctx"),
            P("slab", "ctx"),
            P(),
            P(),
            P(),
            P(None, "slab"),
            P("slab"),
        ),
        check_vma=False,
    )
```
